32 devices in a mesh: replica: 2 (over y), fsdp: 16 (over z, x, core).
Axes of the slice: x: 2, y: 2, z: 4, core: 2. Of those that a mesh axis runs over, the one named last changes fastest.
Arguments:
- tokens: bfloat16 [2, 2048, 6144], P('replica', 'fsdp'), may hold values from -6 to 6
- grad_out: bfloat16 [2, 2048, 6144], P('replica', 'fsdp'), may hold values from -6 to 6
- expert_ids: int32 [2, 2048, 2], P('replica', 'fsdp'), may hold values from 0 to 7, as said below
- gate_share: float32 [2, 2048], P('replica', 'fsdp'), may hold values from 0.05 to 0.95
- up_weight: bfloat16 [2, 6144, 8192], P('replica', None, 'fsdp'), may hold values from -0.078125 to 0.078125
- down_weight: bfloat16 [2, 8192, 6144], P('replica', 'fsdp'), may hold values from -0.0625 to 0.0625
- local_keys: float32 [2, 6144, 512], P('replica', 'fsdp'), may hold values from -6 to 6
- outer_keys: float32 [6144, 512], P('fsdp'), may hold values from -6 to 6
- momentum: float32 [6144, 512], P('fsdp', 'replica'), may hold values from -4 to 4
Outputs:
- input_grad: bfloat16 [2, 2048, 6144], P('replica', 'fsdp')
- new_outer: float32 [6144, 512], P('fsdp')
- new_momentum: float32 [6144, 512], P('fsdp', 'replica')
- outer_copy: bfloat16 [6144, 512], P('fsdp')
The draws below stay inside these ranges and needn't reach their ends.
Inputs may be any that keep to these rules, and one draw needn't show every extreme that they name: `expert_ids`: every token names two different experts. In each replica, each device's 128 consecutive tokens hold exactly 16 that name expert 0.
All inputs are finite; a program needn't handle non-finite values.
Results may differ from the reference program's by a relative error of at most 0.0049.
Values may be sent and summed in bfloat16 or wider, within the bound.
A program may use at most 128 MiB of HBM per device.

```python
import jax
import jax.numpy as jnp
from jax import lax

D = 6144
FF = 8192
KV = 512
EXPERTS = 8
CAP = 16
TOK_DEV = 128
TOKENS = 2048
REPLICAS = 2
N_REPLICA = 2
N_FSDP = 16


def draw_expert_ids(key, part):
    key = jax.random.fold_in(key, 11)
    blocks = REPLICAS * N_FSDP
    keys = jax.random.split(jax.random.fold_in(key, 1), blocks)
    orders = jax.vmap(lambda one: jax.random.permutation(one, TOK_DEV))(keys)
    ranks = jnp.argsort(orders, axis=1)
    routed = (ranks < CAP).reshape(REPLICAS, TOKENS)
    slot = jax.random.randint(jax.random.fold_in(key, 2), (REPLICAS, TOKENS), 0, 2)
    other = jax.random.randint(jax.random.fold_in(key, 3), (REPLICAS, TOKENS), 1, EXPERTS)
    offset = jax.random.randint(jax.random.fold_in(key, 4), (REPLICAS, TOKENS), 1, EXPERTS - 1)
    second = 1 + (other - 1 + offset) % (EXPERTS - 1)
    first_id = jnp.where(routed, jnp.where(slot == 0, 0, other), other)
    second_id = jnp.where(routed, jnp.where(slot == 0, other, 0), second)
    return jnp.stack([first_id, second_id], axis=-1).astype(jnp.int32)


def strengthened(array, rng, source, target, parts, factor):
    def block_of(axis_at):
        return (jnp.arange(array.shape[axis_at]) // (array.shape[axis_at] // parts)).reshape((-1,) + (1,) * (array.ndim - 1 - axis_at))

    one_side = jax.random.permutation(rng, parts)[block_of(target)]
    second = (block_of(target) + parts // 2) % parts
    return jnp.where((block_of(source) == one_side) | (block_of(source) == second), factor * array, array)


def shard_levels(own_key, shape, shards, smallest, high):
    level, own = 1.0, jax.random.fold_in(own_key, 6)
    for axis_at, shards_of in shards:
        heights = jnp.exp(jax.random.uniform(jax.random.fold_in(own, axis_at), (shards_of,), jnp.float32, smallest / len(shards), high / len(shards)))
        level = level * jnp.repeat(heights, shape[axis_at] // shards_of).reshape([-1 if axis == axis_at else 1 for axis in range(len(shape))])
    return level


def bell_draw(stream_key, shape, spread, reach, cuts=(), kind=jnp.bfloat16):
    values = jax.random.normal(stream_key, shape, jnp.float32) * spread
    if len(cuts) > 0:
        values = shard_levels(stream_key, shape, cuts, -0.22, 0.18) * values
    return jnp.clip(values, min=-reach, max=reach).astype(kind)


def noise_with(own_key, shape, deviation, bound, cuts, heavy, dtype=jnp.bfloat16):
    entries = deviation * jax.random.normal(own_key, shape, jnp.float32)
    if cuts:
        entries = entries * shard_levels(own_key, shape, cuts, -0.22, 0.18)
    return jnp.clip(strengthened(entries, jax.random.fold_in(own_key, 3), *heavy), -bound, bound).astype(dtype)


def setup_inputs(seed: int = 0) -> dict:
    streams_of = jax.random.split(jax.random.key(seed), 10)
    return {
        "tokens": bell_draw(streams_of[0], (REPLICAS, TOKENS, D), 1.0, 6.0, ((0, 2), (1, 16))),
        "grad_out": bell_draw(streams_of[1], (REPLICAS, TOKENS, D), 1.0, 6.0, ((0, 2), (1, 16))),
        "expert_ids": draw_expert_ids(jax.random.fold_in(streams_of[9], 71), 0),
        "gate_share": jnp.clip(0.05 + 0.9 * jax.random.uniform(streams_of[3], (REPLICAS, TOKENS), jnp.float32) ** shard_levels(streams_of[3], (REPLICAS, TOKENS), ((0, 2), (1, 16)), -0.2, 0.2), 0.05, 0.95),
        "up_weight": bell_draw(streams_of[4], (REPLICAS, D, FF), D ** -0.5, 0.078125, ((0, 2), (2, 16))),
        "down_weight": bell_draw(streams_of[5], (REPLICAS, FF, D), FF ** -0.5, 0.0625, ((0, 2), (1, 16))),
        "local_keys": noise_with(streams_of[6], (REPLICAS, D, KV), 1.0, 6.0, ((0, 2), (1, 16)), (0, 2, 2, 2.0), jnp.float32),
        "outer_keys": bell_draw(streams_of[7], (D, KV), 1.0, 6.0, ((0, 16),), jnp.float32),
        "momentum": bell_draw(streams_of[8], (D, KV), 0.5, 4.0, ((0, 16), (1, 2)), jnp.float32),
    }


outer_beta = 0.9
outer_rate = 0.7


def one_replica(tokens_r, grads_r, ids_r, share_r, up_r, down_r):
    first = ids_r[:, 0] == 0
    second = ids_r[:, 1] == 0
    coef = jnp.where(first, share_r, jnp.where(second, 1.0 - share_r, 0.0)).astype(jnp.float32)
    picked = jnp.nonzero(first | second, size=N_FSDP * CAP)[0].astype(jnp.int32)
    rows_in = tokens_r[picked]
    rows_grad = grads_r[picked]
    pre = jnp.dot(rows_in, up_r, preferred_element_type=jnp.float32)
    back = lax.dot_general(rows_grad, down_r, (((1,), (1,)), ((), ())), preferred_element_type=jnp.float32)
    sig = jax.nn.sigmoid(pre)
    hidden_grad = (back * sig * (1.0 + pre * (1.0 - sig))).astype(jnp.bfloat16)
    part = lax.dot_general(hidden_grad, up_r, (((1,), (1,)), ((), ())), preferred_element_type=jnp.float32)
    result = (coef[picked][:, None] * part).astype(jnp.bfloat16)
    return jnp.zeros(tokens_r.shape, jnp.bfloat16).at[picked].set(result)


def reference(tokens, grad_out, expert_ids, gate_share, up_weight, down_weight, local_keys, outer_keys, momentum):
    pieces = []
    for replica in range(N_REPLICA):
        pieces.append(one_replica(tokens[replica], grad_out[replica], expert_ids[replica], gate_share[replica], up_weight[replica], down_weight[replica]))
    input_grad = jnp.stack(pieces, axis=0)
    pseudo = jnp.sum(outer_keys[None, :, :] - local_keys, axis=0) / N_REPLICA
    new_momentum = outer_beta * momentum + pseudo
    new_outer = outer_keys - outer_rate * (pseudo + outer_beta * new_momentum)
    return input_grad, new_outer, new_momentum, new_outer.astype(jnp.bfloat16)
```

```python
import functools

import jax
import jax.numpy as jnp
from jax import lax
from jax.experimental import pallas as pl
from jax.experimental.pallas import tpu as pltpu
from jax.sharding import PartitionSpec as P

CAP = 16
MAJOR = 4
PIECES = 8
KEY_PIECES = 8

outer_beta = 0.9
outer_rate = 0.7

MESH = pl.DeviceIdType.MESH


def dot_nn(left, right):
    return jnp.dot(left, right, preferred_element_type=jnp.float32)


def dot_nt(left, right):
    return lax.dot_general(
        left, right, (((1,), (1,)), ((), ())), preferred_element_type=jnp.float32
    )


def staged(count, stages):
    def step(t, carry):
        for lag, stage in stages:
            piece = t - lag

            @pl.when((piece >= 0) & (piece < count))
            def _():
                stage(piece)

        return carry

    lax.fori_loop(0, count + max(lag for lag, _ in stages), step, 0)


def kernel(
    R,
    A,
    B,
    K,
    ids_ref,
    share_ref,
    tok_ref,
    grad_ref,
    up_ref,
    down_ref,
    local_ref,
    mom_ref,
    res_ref,
    sel_out_ref,
    local_all,
    mom_all,
    src,
    buf,
    upv,
    downv,
    sel_ref,
    coef_ref,
    pre_ref,
    back_ref,
    hid_ref,
    part,
    sib_out,
    sib_in,
    x_out,
    x_in,
    z_out,
    z_in,
    src_sem,
    up_sem,
    down_sem,
    own_sem,
    y_send,
    y_recv,
    gz_send,
    gz_recv,
    gx_send,
    gx_recv,
    gs_send,
    gs_recv,
    rs_send,
    rs_recv,
    rx_send,
    rx_recv,
    rz_send,
    rz_recv,
):
    r = lax.axis_index("replica")
    me = lax.axis_index("fsdp")
    c = lax.rem(me, 2)
    b = lax.rem(me // 2, B)
    a = me // (2 * B)
    NP = 2 * K
    width = src.shape[-1]
    column = A * CAP
    half = B * column

    def at(a_, b_, c_):
        return (r, (a_ * B + b_) * 2 + c_)

    sibling = at(a, b, 1 - c)
    z_peers = [at(lax.rem(a + j, A), b, c) for j in range(1, A)]
    x_peers = [at(a, lax.rem(b + j, B), c) for j in range(1, B)]
    y_peers = [(lax.rem(r + j, R), me) for j in range(1, R)]

    for k in range(K):
        cols = pl.ds(k * width, width)
        pltpu.make_async_copy(tok_ref.at[:, cols], src.at[k], src_sem.at[k]).start()
    for k in range(K):
        cols = pl.ds(k * width, width)
        pltpu.make_async_copy(up_ref.at[cols], upv.at[k], up_sem.at[k]).start()
    for k in range(K):
        cols = pl.ds(k * width, width)
        pltpu.make_async_copy(grad_ref.at[:, cols], src.at[K + k], src_sem.at[K + k]).start()
    for k in range(K):
        cols = pl.ds(k * width, width)
        pltpu.make_async_copy(down_ref.at[:, cols], downv.at[k], down_sem.at[k]).start()
    own_local = pltpu.make_async_copy(local_ref, local_all.at[r], own_sem.at[0])
    own_mom = pltpu.make_async_copy(mom_ref, mom_all.at[r], own_sem.at[1])
    own_local.start()
    own_mom.start()

    barrier = pltpu.get_barrier_semaphore()
    peers = [sibling] + z_peers + x_peers + y_peers
    for peer in peers:
        pl.semaphore_signal(barrier, inc=1, device_id=peer, device_id_type=MESH)

    T = ids_ref.shape[0]
    ids = ids_ref[...]
    first = (ids[:, 0:1] == 0).astype(jnp.float32)
    second = (ids[:, 1:2] == 0).astype(jnp.float32)
    named = jnp.broadcast_to(first + second, (T, T))
    row = lax.broadcasted_iota(jnp.int32, (T, T), 0)
    col = lax.broadcasted_iota(jnp.int32, (T, T), 1)
    below = jnp.where(col < row, 1.0, 0.0).astype(jnp.bfloat16)
    rank = dot_nn(below, named.astype(jnp.bfloat16))
    sel_t = jnp.where((rank == col.astype(jnp.float32)) & (named > 0.5), 1.0, 0.0)
    sel_out_ref[...] = sel_t.astype(jnp.bfloat16)
    sel = sel_t.T
    sel_ref[...] = sel[:CAP].astype(jnp.bfloat16)
    first_row = jnp.broadcast_to(first, (T, T)).T
    share = share_ref[...]
    coef = jnp.where(first_row[:CAP] > 0.5, share, 1.0 - share)
    coef_ref[...] = jnp.broadcast_to(
        jnp.sum(sel[:CAP] * coef, axis=1, keepdims=True), coef_ref.shape
    )
    pre_ref[...] = jnp.zeros_like(pre_ref)
    back_ref[...] = jnp.zeros_like(back_ref)

    pl.semaphore_wait(barrier, len(peers))

    def remote(source, target, send, recv, peer):
        return pltpu.make_async_remote_copy(
            src_ref=source,
            dst_ref=target,
            send_sem=send,
            recv_sem=recv,
            device_id=peer,
            device_id_type=MESH,
        )

    def rows_of(b_):
        return pl.ds(pl.multiple_of((c * B + b_) * column, column), column)

    def gz(p):
        mine = buf.at[p, pl.ds(pl.multiple_of((c * B + b) * column + a * CAP, CAP), CAP)]
        return [
            remote(mine, mine, gz_send.at[p, j], gz_recv.at[p, j], z_peers[j])
            for j in range(A - 1)
        ]

    def gx(p):
        mine = buf.at[p, rows_of(b)]
        return [
            remote(mine, mine, gx_send.at[p, j], gx_recv.at[p, j], x_peers[j])
            for j in range(B - 1)
        ]

    def gs(p, j):
        part_of = buf.at[p, rows_of(lax.rem(b + j, B))]
        return remote(part_of, part_of, gs_send.at[p, j], gs_recv.at[p, j], sibling)

    key_rows = local_ref.shape[0] // KEY_PIECES

    def ys(p):
        rows = pl.ds(pl.multiple_of(p * key_rows, 8), key_rows)
        copies = []
        for j in range(R - 1):
            copies.append(
                remote(local_ref.at[rows], local_all.at[r, rows], y_send.at[p, j, 0], y_recv.at[p, j, 0], y_peers[j])
            )
            copies.append(
                remote(mom_ref.at[rows], mom_all.at[r, rows], y_send.at[p, j, 1], y_recv.at[p, j, 1], y_peers[j])
            )
        return copies

    def pick(p):
        pltpu.make_async_copy(tok_ref.at[:, pl.ds(0, width)], src.at[p], src_sem.at[p]).wait()
        rows = pl.ds(pl.multiple_of((c * B + b) * column + a * CAP, CAP), CAP)
        buf[p, rows, :] = dot_nn(sel_ref[...], src[p]).astype(jnp.bfloat16)
        for copy in gz(p):
            copy.start()

        @pl.when(p < KEY_PIECES)
        def _():
            for copy in ys(p):
                copy.start()

    def across(p):
        for copy in gz(p):
            copy.wait_recv()
        for copy in gx(p):
            copy.start()
        gs(p, 0).start()

    def aside(p):
        for j, copy in enumerate(gx(p)):
            copy.wait_recv()
            gs(p, B - 1 - j).start()

    def multiply(p):
        for j in range(B):
            gs(p, j).wait_recv()

        @pl.when(p < K)
        def _():
            pltpu.make_async_copy(up_ref.at[pl.ds(0, width)], upv.at[p], up_sem.at[p]).wait()
            pre_ref[...] += dot_nn(buf[p], upv[p])

        @pl.when(p >= K)
        def _():
            k = p - K
            pltpu.make_async_copy(
                down_ref.at[:, pl.ds(0, width)], downv.at[k], down_sem.at[k]
            ).wait()
            back_ref[...] += dot_nt(buf[p], downv[k])

    staged(NP, [(0, pick), (2, across), (4, aside), (5, multiply)])

    pre = pre_ref[...]
    sig = jax.nn.sigmoid(pre)
    hid_ref[...] = (back_ref[...] * sig * (1.0 + pre * (1.0 - sig))).astype(jnp.bfloat16)

    own_half = pl.ds(pl.multiple_of(c * half, half), half)
    other_half = pl.ds(pl.multiple_of((1 - c) * half, half), half)

    def rs(q):
        return remote(sib_out.at[q], sib_in.at[q], rs_send.at[q], rs_recv.at[q], sibling)

    def rx(q):
        return [
            remote(x_out.at[q, j], x_in.at[q, j], rx_send.at[q, j], rx_recv.at[q, j], x_peers[j])
            for j in range(B - 1)
        ]

    def rz(q):
        return [
            remote(z_out.at[q, j], z_in.at[q, j], rz_send.at[q, j], rz_recv.at[q, j], z_peers[j])
            for j in range(A - 1)
        ]

    def produce(q):
        part[q] = dot_nt(hid_ref[...], upv[q])
        sib_out[q] = part[q, other_half, :].astype(jnp.bfloat16)
        rs(q).start()

    def pair(q):
        rs(q).wait_recv()
        for j, copy in enumerate(rx(q)):
            b_ = lax.rem(b + j + 1, B)
            there = pl.ds(pl.multiple_of(b_ * column, column), column)
            mine = part[q, pl.ds(pl.multiple_of(c * half + b_ * column, column), column), :]
            x_out[q, j] = (mine + sib_in[q, there, :].astype(jnp.float32)).astype(jnp.bfloat16)
            copy.start()

    def chain(q):
        here = pl.ds(pl.multiple_of(b * column, column), column)
        mine = pl.ds(pl.multiple_of(c * half + b * column, column), column)
        total = part[q, mine, :] + sib_in[q, here, :].astype(jnp.float32)
        for j, copy in enumerate(rx(q)):
            copy.wait_recv()
            total = total + x_in[q, j].astype(jnp.float32)
        part[q, mine, :] = total
        for j, copy in enumerate(rz(q)):
            a_ = lax.rem(a + j + 1, A)
            rows = pl.ds(pl.multiple_of(c * half + b * column + a_ * CAP, CAP), CAP)
            z_out[q, j] = part[q, rows, :].astype(jnp.bfloat16)
            copy.start()

    def finish(q):
        rows = pl.ds(pl.multiple_of(c * half + b * column + a * CAP, CAP), CAP)
        total = part[q, rows, :]
        for j, copy in enumerate(rz(q)):
            copy.wait_recv()
            total = total + z_in[q, j].astype(jnp.float32)
        cols = pl.ds(pl.multiple_of(q * width, 128), width)
        res_ref[:, cols] = (coef_ref[:, 0:1] * total).astype(jnp.bfloat16)

    staged(K, [(0, produce), (1, pair), (3, chain), (5, finish)])

    def sent_gather(p, carry):
        for copy in gz(p) + gx(p) + [gs(p, j) for j in range(B)]:
            copy.wait_send()
        return carry

    def sent_reduce(q, carry):
        for copy in [rs(q)] + rx(q) + rz(q):
            copy.wait_send()
        return carry

    def keys_done(p, carry):
        for copy in ys(p):
            copy.wait()
        return carry

    lax.fori_loop(0, NP, sent_gather, 0)
    lax.fori_loop(0, K, sent_reduce, 0)
    lax.fori_loop(0, KEY_PIECES, keys_done, 0)
    own_local.wait()
    own_mom.wait()


def exchange(R, F, ids, share, tokens, grads, up, down, local, momentum):
    A = MAJOR
    B = F // (2 * A)
    K = PIECES
    D = tokens.shape[1]
    H = up.shape[1]
    T = tokens.shape[0]
    width = D // K
    rows = F * CAP
    column = A * CAP
    half = B * column
    dma = pltpu.SemaphoreType.DMA
    vmem = pl.BlockSpec(memory_space=pltpu.VMEM)
    hbm = pl.BlockSpec(memory_space=pl.ANY)
    return pl.pallas_call(
        functools.partial(kernel, R, A, B, K),
        out_shape=(
            jax.ShapeDtypeStruct((CAP, D), jnp.bfloat16),
            jax.ShapeDtypeStruct((T, T), jnp.bfloat16),
            jax.ShapeDtypeStruct((R,) + local.shape, jnp.float32),
            jax.ShapeDtypeStruct((R,) + momentum.shape, jnp.float32),
        ),
        in_specs=[vmem, vmem, hbm, hbm, hbm, hbm, hbm, hbm],
        out_specs=(vmem, vmem, hbm, hbm),
        scratch_shapes=[
            pltpu.VMEM((2 * K, T, width), jnp.bfloat16),
            pltpu.VMEM((2 * K, rows, width), jnp.bfloat16),
            pltpu.VMEM((K, width, H), jnp.bfloat16),
            pltpu.VMEM((K, H, width), jnp.bfloat16),
            pltpu.VMEM((CAP, T), jnp.bfloat16),
            pltpu.VMEM((CAP, 128), jnp.float32),
            pltpu.VMEM((rows, H), jnp.float32),
            pltpu.VMEM((rows, H), jnp.float32),
            pltpu.VMEM((rows, H), jnp.bfloat16),
            pltpu.VMEM((K, rows, width), jnp.float32),
            pltpu.VMEM((K, half, width), jnp.bfloat16),
            pltpu.VMEM((K, half, width), jnp.bfloat16),
            pltpu.VMEM((K, B - 1, column, width), jnp.bfloat16),
            pltpu.VMEM((K, B - 1, column, width), jnp.bfloat16),
            pltpu.VMEM((K, A - 1, CAP, width), jnp.bfloat16),
            pltpu.VMEM((K, A - 1, CAP, width), jnp.bfloat16),
            dma((2 * K,)),
            dma((K,)),
            dma((K,)),
            dma((2,)),
            dma((KEY_PIECES, R - 1, 2)),
            dma((KEY_PIECES, R - 1, 2)),
            dma((2 * K, A - 1)),
            dma((2 * K, A - 1)),
            dma((2 * K, B - 1)),
            dma((2 * K, B - 1)),
            dma((2 * K, B)),
            dma((2 * K, B)),
            dma((K,)),
            dma((K,)),
            dma((K, B - 1)),
            dma((K, B - 1)),
            dma((K, A - 1)),
            dma((K, A - 1)),
        ],
        compiler_params=pltpu.CompilerParams(
            collective_id=0, has_side_effects=True, vmem_limit_bytes=60 * 1024 * 1024
        ),
        cost_estimate=pl.CostEstimate(
            flops=6 * rows * D * H, bytes_accessed=8 * D * H, transcendentals=rows * H
        ),
    )(ids, share, tokens, grads, up, down, local, momentum)


def per_device(
    R,
    F,
    tokens,
    grad_out,
    expert_ids,
    gate_share,
    up_weight,
    down_weight,
    local_keys,
    outer_keys,
    momentum,
):
    result, sel, local_all, mom_all = exchange(
        R,
        F,
        expert_ids[0],
        gate_share,
        tokens[0],
        grad_out[0],
        up_weight[0],
        down_weight[0],
        local_keys[0],
        momentum,
    )
    input_grad = jnp.dot(
        sel[:, :CAP], result, preferred_element_type=jnp.float32
    ).astype(jnp.bfloat16)
    pseudo = outer_keys - local_all[0]
    for one in range(1, R):
        pseudo = pseudo + (outer_keys - local_all[one])
    pseudo = pseudo / R
    every = jnp.concatenate([mom_all[one] for one in range(R)], axis=1)
    moved = outer_beta * every + pseudo
    new_outer = outer_keys - outer_rate * (pseudo + outer_beta * moved)
    width = momentum.shape[1]
    new_momentum = lax.dynamic_slice_in_dim(moved, lax.axis_index("replica") * width, width, 1)
    return (input_grad[None], new_outer, new_momentum, new_outer.astype(jnp.bfloat16))


def solution(mesh):
    placed = (
        P("replica", "fsdp", None),
        P("replica", "fsdp", None),
        P("replica", "fsdp", None),
        P("replica", "fsdp"),
        P("replica", None, "fsdp"),
        P("replica", "fsdp", None),
        P("replica", "fsdp", None),
        P("fsdp", None),
        P("fsdp", "replica"),
    )
    return jax.shard_map(
        functools.partial(per_device, mesh.shape["replica"], mesh.shape["fsdp"]),
        mesh=mesh,
        in_specs=placed,
        out_specs=(
            P("replica", "fsdp", None),
            P("fsdp", None),
            P("fsdp", "replica"),
            P("fsdp", None),
        ),
        check_vma=False,
    )
```

```python
import functools

import jax
import jax.numpy as jnp
from jax import lax
from jax.experimental import pallas as pl
from jax.experimental.pallas import tpu as pltpu
from jax.sharding import PartitionSpec as P

CAP = 16
MAJOR = 4
PIECES = 8
BACK_PIECES = 12
KEY_PIECES = 8
TAIL_STEPS = 4

outer_beta = 0.9
outer_rate = 0.7

MESH = pl.DeviceIdType.MESH


def dot_nn(left, right):
    return jnp.dot(left, right, preferred_element_type=jnp.float32)


def dot_nt(left, right):
    return lax.dot_general(
        left, right, (((1,), (1,)), ((), ())), preferred_element_type=jnp.float32
    )


def staged(count, stages):
    def step(t, carry):
        for lag, stage in stages:
            piece = t - lag

            @pl.when((piece >= 0) & (piece < count))
            def _():
                stage(piece)

        return carry

    lax.fori_loop(0, count + max(lag for lag, _ in stages), step, 0)


def kernel(
    R,
    B,
    K,
    KR,
    ids_ref,
    share_ref,
    tok_ref,
    grad_ref,
    up_ref,
    down_ref,
    local_ref,
    mom_ref,
    res_ref,
    sel_out_ref,
    local_all,
    mom_all,
    src,
    buf,
    upv,
    downv,
    sel_ref,
    coef_ref,
    pre_ref,
    back_ref,
    hid_ref,
    part,
    sib_out,
    sib_in,
    x_out,
    x_in,
    n_out,
    n_in,
    m_out,
    m_in,
    d_out,
    d_in,
    src_sem,
    up_sem,
    down_sem,
    own_sem,
    y_send,
    y_recv,
    g_send,
    g_recv,
    r_send,
    r_recv,
):
    A = MAJOR
    r = lax.axis_index("replica")
    me = lax.axis_index("fsdp")
    c = lax.rem(me, 2)
    b = lax.rem(me // 2, B)
    a = me // (2 * B)
    NP = 2 * K
    width = src.shape[-1]
    column = A * CAP
    half = B * column
    a_mate = a + 1 - 2 * lax.rem(a, 2)
    a_diag = lax.rem(a + 2, A)
    a_cross = A - 1 - a
    a_pair = 2 - 2 * (a // 2)

    def at(a_, b_, c_):
        return (r, (a_ * B + b_) * 2 + c_)

    sibling = at(a, b, 1 - c)
    mate = at(a_mate, b, c)
    diag = at(a_diag, b, c)
    x_peers = [at(a, lax.rem(b + j, B), c) for j in range(1, B)]
    y_peers = [(lax.rem(r + j, R), me) for j in range(1, R)]

    for k in range(K):
        cols = pl.ds(k * width, width)
        pltpu.make_async_copy(tok_ref.at[:, cols], src.at[k], src_sem.at[k]).start()
    for k in range(K):
        cols = pl.ds(k * width, width)
        pltpu.make_async_copy(up_ref.at[cols], upv.at[cols], up_sem.at[k]).start()
    for k in range(K):
        cols = pl.ds(k * width, width)
        pltpu.make_async_copy(grad_ref.at[:, cols], src.at[K + k], src_sem.at[K + k]).start()
    for k in range(K):
        cols = pl.ds(k * width, width)
        pltpu.make_async_copy(down_ref.at[:, cols], downv.at[k], down_sem.at[k]).start()
    own_local = pltpu.make_async_copy(local_ref, local_all.at[r], own_sem.at[0])
    own_mom = pltpu.make_async_copy(mom_ref, mom_all.at[r], own_sem.at[1])
    own_local.start()
    own_mom.start()

    barrier = pltpu.get_barrier_semaphore()
    peers = [sibling, mate, diag] + x_peers + y_peers
    for peer in peers:
        pl.semaphore_signal(barrier, inc=1, device_id=peer, device_id_type=MESH)

    T = ids_ref.shape[1]
    first = (ids_ref[0:1, :] == 0).astype(jnp.float32)
    second = (ids_ref[1:2, :] == 0).astype(jnp.float32)
    named = jnp.broadcast_to(first + second, (T, T)).T
    row = lax.broadcasted_iota(jnp.int32, (T, T), 0)
    col = lax.broadcasted_iota(jnp.int32, (T, T), 1)
    below = jnp.where(col < row, 1.0, 0.0).astype(jnp.bfloat16)
    rank = dot_nn(below, named.astype(jnp.bfloat16))
    sel_t = jnp.where((rank == col.astype(jnp.float32)) & (named > 0.5), 1.0, 0.0)
    sel_out_ref[...] = sel_t.astype(jnp.bfloat16)
    sel = sel_t.T
    sel_ref[...] = sel[:CAP].astype(jnp.bfloat16)
    share = share_ref[...]
    coef = jnp.where(first > 0.5, share, 1.0 - share)
    coef_ref[...] = jnp.broadcast_to(
        jnp.sum(sel[:CAP] * coef, axis=1, keepdims=True), coef_ref.shape
    )
    pre_ref[...] = jnp.zeros_like(pre_ref)
    back_ref[...] = jnp.zeros_like(back_ref)

    pl.semaphore_wait(barrier, len(peers))

    def remote(source, target, send, recv, peer):
        return pltpu.make_async_remote_copy(
            src_ref=source,
            dst_ref=target,
            send_sem=send,
            recv_sem=recv,
            device_id=peer,
            device_id_type=MESH,
        )

    def block(b_, a_, count=1):
        return pl.ds(pl.multiple_of(((c * B + b_) * A + a_) * CAP, CAP), count * CAP)

    def passed(p, rows, slot, peer):
        ref = buf.at[p, rows]
        return remote(ref, ref, g_send.at[p, slot], g_recv.at[p, slot], peer)

    def g_diag(p):
        return passed(p, block(b, a), 0, diag)

    def g_mate(p):
        return passed(p, block(b, a), 1, mate)

    def g_cross(p):
        return passed(p, block(b, a_diag), 2, mate)

    def g_sib(p, j):
        return passed(p, block(lax.rem(b + j, B), 0, A), 3 + j, sibling)

    def g_x_own(p, j):
        return passed(p, block(b, a), 3 + B + 3 * j, x_peers[j])

    def g_x_pair(p, j):
        return passed(p, block(b, a_pair, 2), 4 + B + 3 * j, x_peers[j])

    def g_x_mate(p, j):
        return passed(p, block(b, a_mate), 5 + B + 3 * j, x_peers[j])

    def g_turn(p, j):
        return passed(p, block(lax.rem(b + B - 1 - j, B), a), 5 + B + 3 * j, mate)

    key_rows = local_ref.shape[0] // KEY_PIECES

    def ys(p):
        rows = pl.ds(pl.multiple_of(p * key_rows, 8), key_rows)
        copies = []
        for j in range(R - 1):
            copies.append(
                remote(local_ref.at[rows], local_all.at[r, rows], y_send.at[p, j, 0], y_recv.at[p, j, 0], y_peers[j])
            )
            copies.append(
                remote(mom_ref.at[rows], mom_all.at[r, rows], y_send.at[p, j, 1], y_recv.at[p, j, 1], y_peers[j])
            )
        return copies

    def even(p, then, otherwise):
        pl.when(lax.rem(p, 2) == 0)(then)
        pl.when(lax.rem(p, 2) == 1)(otherwise)

    def pick(p):
        pltpu.make_async_copy(tok_ref.at[:, pl.ds(0, width)], src.at[p], src_sem.at[p]).wait()
        buf[p, block(b, a), :] = dot_nn(sel_ref[...], src[p]).astype(jnp.bfloat16)
        g_diag(p).start()
        for j in range(B - 1):
            g_x_own(p, j).start()
        g_mate(p).start()

        @pl.when(p < KEY_PIECES)
        def _():
            for copy in ys(p):
                copy.start()

    def second_round(p):
        g_diag(p).wait_recv()
        g_cross(p).start()
        g_mate(p).wait_recv()

        @pl.when(lax.rem(p, 2) == 0)
        def _():
            for j in range(B - 1):
                g_x_mate(p, j).start()

    def across(p):
        g_cross(p).wait_recv()
        for j in range(B - 1):
            g_x_pair(p, j).start()
        for j in range(B - 1):
            g_x_own(p, j).wait_recv()

        @pl.when(lax.rem(p, 2) == 1)
        def _():
            for j in range(B - 1):
                g_turn(p, j).start()

        g_sib(p, 0).start()

    def aside(p):
        def by_x():
            for j in range(B - 1):
                g_x_mate(p, j).wait_recv()

        def by_mate():
            for j in range(B - 1):
                g_turn(p, j).wait_recv()

        for j in range(B - 1):
            g_x_pair(p, j).wait_recv()
        even(p, by_x, by_mate)
        for j in range(1, B):
            g_sib(p, j).start()

    def multiply(p):
        for j in range(B):
            g_sib(p, j).wait_recv()

        @pl.when(p < K)
        def _():
            rows = pl.ds(pl.multiple_of(p * width, width), width)
            pltpu.make_async_copy(up_ref.at[pl.ds(0, width)], upv.at[rows], up_sem.at[p]).wait()
            pre_ref[...] += dot_nn(buf[p], upv[rows, :])

        @pl.when(p >= K)
        def _():
            k = p - K
            pltpu.make_async_copy(
                down_ref.at[:, pl.ds(0, width)], downv.at[k], down_sem.at[k]
            ).wait()
            back_ref[...] += dot_nt(buf[p], downv[k])

    staged(NP, [(0, pick), (2, second_round), (3, across), (5, aside), (6, multiply)])

    pre = pre_ref[...]
    sig = jax.nn.sigmoid(pre)
    hid_ref[...] = (back_ref[...] * sig * (1.0 + pre * (1.0 - sig))).astype(jnp.bfloat16)

    wide = part.shape[-1]
    other_half = pl.ds(pl.multiple_of((1 - c) * half, half), half)

    def inner(a_, count=1):
        return pl.ds(pl.multiple_of(a_ * CAP, CAP), count * CAP)

    def back(source, target, q, slot, peer):
        return remote(source, target, r_send.at[q, slot], r_recv.at[q, slot], peer)

    def r_sib(q):
        return back(sib_out.at[q], sib_in.at[q], q, 0, sibling)

    def r_mate(q):
        return back(m_out.at[q], m_in.at[q], q, 1, mate)

    def r_diag(q):
        return back(d_out.at[q], d_in.at[q], q, 2, diag)

    def r_x_all(q, j):
        return back(x_out.at[q, j], x_in.at[q, j], q, 3 + 3 * j, x_peers[j])

    def r_x_pair(q, j):
        rows = inner(a_pair, 2)
        return back(x_out.at[q, j, rows], x_in.at[q, j, rows], q, 3 + 3 * j, x_peers[j])

    def r_x_own(q, j):
        rows = inner(a)
        return back(x_out.at[q, j, rows], x_in.at[q, j, rows], q, 4 + 3 * j, x_peers[j])

    def r_turn(q, j):
        return back(n_out.at[q, j], n_in.at[q, j], q, 5 + 3 * j, mate)

    def produce(q):
        rows = pl.ds(pl.multiple_of(q * wide, wide), wide)
        part[q] = dot_nt(hid_ref[...], upv[rows, :])
        sib_out[q] = part[q, other_half, :].astype(jnp.bfloat16)
        r_sib(q).start()

    def pair(q):
        r_sib(q).wait_recv()
        for j in range(B - 1):
            b_ = lax.rem(b + j + 1, B)
            there = pl.ds(pl.multiple_of(b_ * column, column), column)
            mine = block(b_, 0, A)
            total = part[q, mine, :] + sib_in[q, there, :].astype(jnp.float32)
            part[q, mine, :] = total

            def whole():
                x_out[q, j] = part[q, mine, :].astype(jnp.bfloat16)
                r_x_all(q, j).start()

            def split():
                n_out[q, j] = part[q, block(b_, a_mate), :].astype(jnp.bfloat16)
                r_turn(q, j).start()
                x_out[q, j, inner(a_pair, 2), :] = part[q, block(b_, a_pair, 2), :].astype(
                    jnp.bfloat16
                )
                r_x_pair(q, j).start()

            even(q, whole, split)
        here = pl.ds(pl.multiple_of(b * column, column), column)
        mine = block(b, 0, A)
        part[q, mine, :] = part[q, mine, :] + sib_in[q, here, :].astype(jnp.float32)

    def turned(q):
        @pl.when(lax.rem(q, 2) == 1)
        def _():
            for j in range(B - 1):
                b_ = lax.rem(b + j + 1, B)
                r_turn(q, j).wait_recv()
                x_out[q, j, inner(a), :] = (
                    part[q, block(b_, a), :] + n_in[q, j].astype(jnp.float32)
                ).astype(jnp.bfloat16)
                r_x_own(q, j).start()

    def chain(q):
        def whole():
            mine = block(b, 0, A)
            for j in range(B - 1):
                r_x_all(q, j).wait_recv()
                part[q, mine, :] = part[q, mine, :] + x_in[q, j].astype(jnp.float32)

        def split():
            for j in range(B - 1):
                r_x_pair(q, j).wait_recv()
                r_x_own(q, j).wait_recv()
                for b_, rows in ((block(b, a_pair, 2), inner(a_pair, 2)), (block(b, a), inner(a))):
                    part[q, b_, :] = part[q, b_, :] + x_in[q, j, rows, :].astype(jnp.float32)

        even(q, whole, split)
        m_out[q, 0] = part[q, block(b, a_mate), :].astype(jnp.bfloat16)
        m_out[q, 1] = part[q, block(b, a_cross), :].astype(jnp.bfloat16)
        r_mate(q).start()

    def far(q):
        r_mate(q).wait_recv()
        d_out[q] = (part[q, block(b, a_diag), :] + m_in[q, 1].astype(jnp.float32)).astype(
            jnp.bfloat16
        )
        r_diag(q).start()

    def finish(q):
        r_diag(q).wait_recv()
        total = part[q, block(b, a), :] + m_in[q, 0].astype(jnp.float32)
        total = total + d_in[q].astype(jnp.float32)
        cols = pl.ds(pl.multiple_of(q * wide, 128), wide)
        res_ref[:, cols] = (coef_ref[:, 0:1] * total).astype(jnp.bfloat16)

    staged(KR, [(0, produce), (1, pair), (2, turned), (4, chain), (5, far), (6, finish)])

    def sent_gather(p, carry):
        copies = [g_diag(p), g_mate(p), g_cross(p)]
        for j in range(B):
            copies.append(g_sib(p, j))
        for j in range(B - 1):
            copies += [g_x_own(p, j), g_x_pair(p, j), g_x_mate(p, j)]
        for copy in copies:
            copy.wait_send()
        return carry

    def sent_reduce(q, carry):
        for copy in (r_sib(q), r_mate(q), r_diag(q)):
            copy.wait_send()

        def whole():
            for j in range(B - 1):
                r_x_all(q, j).wait_send()

        def split():
            for j in range(B - 1):
                for copy in (r_x_pair(q, j), r_x_own(q, j), r_turn(q, j)):
                    copy.wait_send()

        even(q, whole, split)
        return carry

    def keys_done(p, carry):
        for copy in ys(p):
            copy.wait()
        return carry

    lax.fori_loop(0, NP, sent_gather, 0)
    lax.fori_loop(0, KR, sent_reduce, 0)
    lax.fori_loop(0, KEY_PIECES, keys_done, 0)
    own_local.wait()
    own_mom.wait()


def exchange(R, F, ids, share, tokens, grads, up, down, local, momentum):
    A = MAJOR
    B = F // (2 * A)
    K = PIECES
    KR = BACK_PIECES
    T, D = tokens.shape
    H = up.shape[1]
    width = D // K
    wide = D // KR
    rows = F * CAP
    column = A * CAP
    half = B * column
    dma = pltpu.SemaphoreType.DMA
    vmem = pl.BlockSpec(memory_space=pltpu.VMEM)
    hbm = pl.BlockSpec(memory_space=pl.ANY)
    return pl.pallas_call(
        functools.partial(kernel, R, B, K, KR),
        out_shape=(
            jax.ShapeDtypeStruct((CAP, D), jnp.bfloat16),
            jax.ShapeDtypeStruct((T, T), jnp.bfloat16),
            jax.ShapeDtypeStruct((R,) + local.shape, jnp.float32),
            jax.ShapeDtypeStruct((R,) + momentum.shape, jnp.float32),
        ),
        in_specs=[vmem, vmem, hbm, hbm, hbm, hbm, hbm, hbm],
        out_specs=(vmem, vmem, hbm, hbm),
        scratch_shapes=[
            pltpu.VMEM((2 * K, T, width), jnp.bfloat16),
            pltpu.VMEM((2 * K, rows, width), jnp.bfloat16),
            pltpu.VMEM((D, H), jnp.bfloat16),
            pltpu.VMEM((K, H, width), jnp.bfloat16),
            pltpu.VMEM((CAP, T), jnp.bfloat16),
            pltpu.VMEM((CAP, 128), jnp.float32),
            pltpu.VMEM((rows, H), jnp.float32),
            pltpu.VMEM((rows, H), jnp.float32),
            pltpu.VMEM((rows, H), jnp.bfloat16),
            pltpu.VMEM((KR, rows, wide), jnp.float32),
            pltpu.VMEM((KR, half, wide), jnp.bfloat16),
            pltpu.VMEM((KR, half, wide), jnp.bfloat16),
            pltpu.VMEM((KR, B - 1, column, wide), jnp.bfloat16),
            pltpu.VMEM((KR, B - 1, column, wide), jnp.bfloat16),
            pltpu.VMEM((KR, B - 1, CAP, wide), jnp.bfloat16),
            pltpu.VMEM((KR, B - 1, CAP, wide), jnp.bfloat16),
            pltpu.VMEM((KR, 2, CAP, wide), jnp.bfloat16),
            pltpu.VMEM((KR, 2, CAP, wide), jnp.bfloat16),
            pltpu.VMEM((KR, CAP, wide), jnp.bfloat16),
            pltpu.VMEM((KR, CAP, wide), jnp.bfloat16),
            dma((2 * K,)),
            dma((K,)),
            dma((K,)),
            dma((2,)),
            dma((KEY_PIECES, R - 1, 2)),
            dma((KEY_PIECES, R - 1, 2)),
            dma((2 * K, 4 * B)),
            dma((2 * K, 4 * B)),
            dma((KR, 3 * B)),
            dma((KR, 3 * B)),
        ],
        compiler_params=pltpu.CompilerParams(
            collective_id=0, has_side_effects=True, vmem_limit_bytes=60 * 1024 * 1024
        ),
        cost_estimate=pl.CostEstimate(
            flops=6 * rows * D * H, bytes_accessed=8 * D * H, transcendentals=rows * H
        ),
    )(ids, share, tokens, grads, up, down, local, momentum)


def tail_kernel(
    R, sel_ref, res_ref, outer_ref, local_ref, mom_ref, grad_ref, new_ref, moved_ref, copy_ref
):
    r = lax.axis_index("replica")
    width = mom_ref.shape[-1]
    grad_ref[...] = dot_nn(sel_ref[:, :CAP], res_ref[...]).astype(jnp.bfloat16)
    for one in range(R):
        cols = slice(one * width, (one + 1) * width)
        outer = outer_ref[:, cols]
        pseudo = outer - local_ref[0, :, cols]
        for other in range(1, R):
            pseudo = pseudo + (outer - local_ref[other, :, cols])
        pseudo = pseudo / R
        moved = outer_beta * mom_ref[one] + pseudo
        new_outer = outer - outer_rate * (pseudo + outer_beta * moved)
        new_ref[:, cols] = new_outer
        copy_ref[:, cols] = new_outer.astype(jnp.bfloat16)

        @pl.when(r == one)
        def _():
            moved_ref[...] = moved


def tail(R, sel, result, outer, local_all, mom_all):
    T = sel.shape[0]
    D = result.shape[1]
    rows, keys = outer.shape
    width = mom_all.shape[2]
    G = TAIL_STEPS
    few, cols = rows // G, D // G
    return pl.pallas_call(
        functools.partial(tail_kernel, R),
        grid=(G,),
        out_shape=(
            jax.ShapeDtypeStruct((T, D), jnp.bfloat16),
            jax.ShapeDtypeStruct((rows, keys), jnp.float32),
            jax.ShapeDtypeStruct((rows, width), jnp.float32),
            jax.ShapeDtypeStruct((rows, keys), jnp.bfloat16),
        ),
        in_specs=[
            pl.BlockSpec((T, T), lambda g: (0, 0)),
            pl.BlockSpec((CAP, cols), lambda g: (0, g)),
            pl.BlockSpec((few, keys), lambda g: (g, 0)),
            pl.BlockSpec((R, few, keys), lambda g: (0, g, 0)),
            pl.BlockSpec((R, few, width), lambda g: (0, g, 0)),
        ],
        out_specs=(
            pl.BlockSpec((T, cols), lambda g: (0, g)),
            pl.BlockSpec((few, keys), lambda g: (g, 0)),
            pl.BlockSpec((few, width), lambda g: (g, 0)),
            pl.BlockSpec((few, keys), lambda g: (g, 0)),
        ),
        compiler_params=pltpu.CompilerParams(vmem_limit_bytes=32 * 1024 * 1024),
    )(sel, result, outer, local_all, mom_all)


def per_device(
    R,
    F,
    tokens,
    grad_out,
    expert_ids,
    gate_share,
    up_weight,
    down_weight,
    local_keys,
    outer_keys,
    momentum,
):
    result, sel, local_all, mom_all = exchange(
        R,
        F,
        expert_ids[0].T,
        gate_share,
        tokens[0],
        grad_out[0],
        up_weight[0],
        down_weight[0],
        local_keys[0],
        momentum,
    )
    input_grad, new_outer, new_momentum, outer_copy = tail(
        R, sel, result, outer_keys, local_all, mom_all
    )
    return (input_grad[None], new_outer, new_momentum, outer_copy)


def solution(mesh):
    placed = (
        P("replica", "fsdp", None),
        P("replica", "fsdp", None),
        P("replica", "fsdp", None),
        P("replica", "fsdp"),
        P("replica", None, "fsdp"),
        P("replica", "fsdp", None),
        P("replica", "fsdp", None),
        P("fsdp", None),
        P("fsdp", "replica"),
    )
    return jax.shard_map(
        functools.partial(per_device, mesh.shape["replica"], mesh.shape["fsdp"]),
        mesh=mesh,
        in_specs=placed,
        out_specs=(
            P("replica", "fsdp", None),
            P("fsdp", None),
            P("fsdp", "replica"),
            P("fsdp", None),
        ),
        check_vma=False,
    )
```

```python
import functools

import jax
import jax.numpy as jnp
from jax import lax
from jax.experimental import pallas as pl
from jax.experimental.pallas import tpu as pltpu
from jax.sharding import PartitionSpec as P

CAP = 16
MAJOR = 4
PIECES = 6
BACK_PIECES = 8
KEY_PIECES = 4
TAIL_STEPS = 4

outer_beta = 0.9
outer_rate = 0.7

MESH = pl.DeviceIdType.MESH


def dot_nn(left, right):
    return jnp.dot(left, right, preferred_element_type=jnp.float32)


def dot_nt(left, right):
    return lax.dot_general(
        left, right, (((1,), (1,)), ((), ())), preferred_element_type=jnp.float32
    )


def staged(count, stages):
    def step(t, carry):
        for lag, stage in stages:
            piece = t - lag

            @pl.when((piece >= 0) & (piece < count))
            def _():
                stage(piece)

        return carry

    lax.fori_loop(0, count + max(lag for lag, _ in stages), step, 0)


def kernel(
    R,
    A,
    B,
    K,
    KR,
    ids_ref,
    share_ref,
    tok_ref,
    grad_ref,
    up_ref,
    down_ref,
    local_ref,
    mom_ref,
    res_ref,
    sel_out_ref,
    local_all,
    mom_all,
    src,
    buf,
    upv,
    downv,
    sel_ref,
    coef_ref,
    pre_ref,
    back_ref,
    hid_ref,
    part,
    sib_out,
    sib_in,
    x_out,
    x_in,
    z_out,
    z_in,
    src_sem,
    up_sem,
    down_sem,
    own_sem,
    y_send,
    y_recv,
    gz_send,
    gz_recv,
    gx_send,
    gx_recv,
    gs_send,
    gs_recv,
    rs_send,
    rs_recv,
    rx_send,
    rx_recv,
    rz_send,
    rz_recv,
):
    r = lax.axis_index("replica")
    me = lax.axis_index("fsdp")
    c = lax.rem(me, 2)
    b = lax.rem(me // 2, B)
    a = me // (2 * B)
    NP = 2 * K
    width = src.shape[-1]
    column = A * CAP
    half = B * column

    def at(a_, b_, c_):
        return (r, (a_ * B + b_) * 2 + c_)

    sibling = at(a, b, 1 - c)
    z_peers = [at(lax.rem(a + j, A), b, c) for j in range(1, A)]
    x_peers = [at(a, lax.rem(b + j, B), c) for j in range(1, B)]
    y_peers = [(lax.rem(r + j, R), me) for j in range(1, R)]

    for k in range(K):
        cols = pl.ds(k * width, width)
        pltpu.make_async_copy(tok_ref.at[:, cols], src.at[k], src_sem.at[k]).start()
    for k in range(K):
        cols = pl.ds(k * width, width)
        pltpu.make_async_copy(up_ref.at[cols], upv.at[cols], up_sem.at[k]).start()
    for k in range(K):
        cols = pl.ds(k * width, width)
        pltpu.make_async_copy(grad_ref.at[:, cols], src.at[K + k], src_sem.at[K + k]).start()
    for k in range(K):
        cols = pl.ds(k * width, width)
        pltpu.make_async_copy(down_ref.at[:, cols], downv.at[k], down_sem.at[k]).start()
    own_local = pltpu.make_async_copy(local_ref, local_all.at[r], own_sem.at[0])
    own_mom = pltpu.make_async_copy(mom_ref, mom_all.at[r], own_sem.at[1])
    own_local.start()
    own_mom.start()

    barrier = pltpu.get_barrier_semaphore()
    peers = [sibling] + z_peers + x_peers + y_peers
    for peer in peers:
        pl.semaphore_signal(barrier, inc=1, device_id=peer, device_id_type=MESH)

    T = ids_ref.shape[1]
    first = (ids_ref[0:1, :] == 0).astype(jnp.float32)
    second = (ids_ref[1:2, :] == 0).astype(jnp.float32)
    named = jnp.broadcast_to(first + second, (T, T)).T
    row = lax.broadcasted_iota(jnp.int32, (T, T), 0)
    col = lax.broadcasted_iota(jnp.int32, (T, T), 1)
    below = jnp.where(col < row, 1.0, 0.0).astype(jnp.bfloat16)
    rank = dot_nn(below, named.astype(jnp.bfloat16))
    sel_t = jnp.where((rank == col.astype(jnp.float32)) & (named > 0.5), 1.0, 0.0)
    sel_out_ref[...] = sel_t.astype(jnp.bfloat16)
    sel = sel_t.T
    sel_ref[...] = sel[:CAP].astype(jnp.bfloat16)
    share = share_ref[...]
    coef = jnp.where(first > 0.5, share, 1.0 - share)
    coef_ref[...] = jnp.broadcast_to(
        jnp.sum(sel[:CAP] * coef, axis=1, keepdims=True), coef_ref.shape
    )
    pre_ref[...] = jnp.zeros_like(pre_ref)
    back_ref[...] = jnp.zeros_like(back_ref)

    pl.semaphore_wait(barrier, len(peers))

    def remote(source, target, send, recv, peer):
        return pltpu.make_async_remote_copy(
            src_ref=source,
            dst_ref=target,
            send_sem=send,
            recv_sem=recv,
            device_id=peer,
            device_id_type=MESH,
        )

    def rows_of(b_):
        return pl.ds(pl.multiple_of((c * B + b_) * column, column), column)

    def gz(p):
        mine = buf.at[p, pl.ds(pl.multiple_of((c * B + b) * column + a * CAP, CAP), CAP)]
        return [
            remote(mine, mine, gz_send.at[p, j], gz_recv.at[p, j], z_peers[j])
            for j in range(A - 1)
        ]

    def gx(p):
        mine = buf.at[p, rows_of(b)]
        return [
            remote(mine, mine, gx_send.at[p, j], gx_recv.at[p, j], x_peers[j])
            for j in range(B - 1)
        ]

    def gs(p, j):
        part_of = buf.at[p, rows_of(lax.rem(b + j, B))]
        return remote(part_of, part_of, gs_send.at[p, j], gs_recv.at[p, j], sibling)

    key_rows = local_ref.shape[0] // KEY_PIECES

    def ys(p):
        rows = pl.ds(pl.multiple_of(p * key_rows, 8), key_rows)
        copies = []
        for j in range(R - 1):
            copies.append(
                remote(local_ref.at[rows], local_all.at[r, rows], y_send.at[p, j, 0], y_recv.at[p, j, 0], y_peers[j])
            )
            copies.append(
                remote(mom_ref.at[rows], mom_all.at[r, rows], y_send.at[p, j, 1], y_recv.at[p, j, 1], y_peers[j])
            )
        return copies

    def pick(p):
        pltpu.make_async_copy(tok_ref.at[:, pl.ds(0, width)], src.at[p], src_sem.at[p]).wait()
        rows = pl.ds(pl.multiple_of((c * B + b) * column + a * CAP, CAP), CAP)
        buf[p, rows, :] = dot_nn(sel_ref[...], src[p]).astype(jnp.bfloat16)
        for copy in gz(p):
            copy.start()

        @pl.when(p < KEY_PIECES)
        def _():
            for copy in ys(p):
                copy.start()

    def across(p):
        for copy in gz(p):
            copy.wait_recv()
        for copy in gx(p):
            copy.start()
        gs(p, 0).start()

    def aside(p):
        for j, copy in enumerate(gx(p)):
            copy.wait_recv()
            gs(p, B - 1 - j).start()

    def multiply(p):
        for j in range(B):
            gs(p, j).wait_recv()

        @pl.when(p < K)
        def _():
            rows = pl.ds(pl.multiple_of(p * width, width), width)
            pltpu.make_async_copy(up_ref.at[pl.ds(0, width)], upv.at[rows], up_sem.at[p]).wait()
            pre_ref[...] += dot_nn(buf[p], upv[rows, :])

        @pl.when(p >= K)
        def _():
            k = p - K
            pltpu.make_async_copy(
                down_ref.at[:, pl.ds(0, width)], downv.at[k], down_sem.at[k]
            ).wait()
            back_ref[...] += dot_nt(buf[p], downv[k])

    def sent(p):
        for copy in gz(p) + gx(p) + [gs(p, j) for j in range(B)]:
            copy.wait_send()

    staged(NP, [(0, pick), (3, across), (5, aside), (6, multiply), (6, sent)])

    pre = pre_ref[...]
    sig = jax.nn.sigmoid(pre)
    hid_ref[...] = (back_ref[...] * sig * (1.0 + pre * (1.0 - sig))).astype(jnp.bfloat16)

    wide = part.shape[-1]
    own_half = pl.ds(pl.multiple_of(c * half, half), half)
    other_half = pl.ds(pl.multiple_of((1 - c) * half, half), half)

    def rs(q):
        return remote(sib_out.at[q], sib_in.at[q], rs_send.at[q], rs_recv.at[q], sibling)

    def rx(q):
        return [
            remote(x_out.at[q, j], x_in.at[q, j], rx_send.at[q, j], rx_recv.at[q, j], x_peers[j])
            for j in range(B - 1)
        ]

    def rz(q):
        return [
            remote(z_out.at[q, j], z_in.at[q, j], rz_send.at[q, j], rz_recv.at[q, j], z_peers[j])
            for j in range(A - 1)
        ]

    def produce(q):
        rows = pl.ds(pl.multiple_of(q * wide, wide), wide)
        part[q] = dot_nt(hid_ref[...], upv[rows, :])
        sib_out[q] = part[q, other_half, :].astype(jnp.bfloat16)
        rs(q).start()

    def pair(q):
        rs(q).wait_recv()
        for j, copy in enumerate(rx(q)):
            b_ = lax.rem(b + j + 1, B)
            there = pl.ds(pl.multiple_of(b_ * column, column), column)
            mine = part[q, pl.ds(pl.multiple_of(c * half + b_ * column, column), column), :]
            x_out[q, j] = (mine + sib_in[q, there, :].astype(jnp.float32)).astype(jnp.bfloat16)
            copy.start()

    def chain(q):
        here = pl.ds(pl.multiple_of(b * column, column), column)
        mine = pl.ds(pl.multiple_of(c * half + b * column, column), column)
        total = part[q, mine, :] + sib_in[q, here, :].astype(jnp.float32)
        for j, copy in enumerate(rx(q)):
            copy.wait_recv()
            total = total + x_in[q, j].astype(jnp.float32)
        part[q, mine, :] = total
        for j, copy in enumerate(rz(q)):
            a_ = lax.rem(a + j + 1, A)
            rows = pl.ds(pl.multiple_of(c * half + b * column + a_ * CAP, CAP), CAP)
            z_out[q, j] = part[q, rows, :].astype(jnp.bfloat16)
            copy.start()

    def finish(q):
        rows = pl.ds(pl.multiple_of(c * half + b * column + a * CAP, CAP), CAP)
        total = part[q, rows, :]
        for j, copy in enumerate(rz(q)):
            copy.wait_recv()
            total = total + z_in[q, j].astype(jnp.float32)
        cols = pl.ds(pl.multiple_of(q * wide, 128), wide)
        res_ref[:, cols] = (coef_ref[:, 0:1] * total).astype(jnp.bfloat16)

    def returned(q):
        for copy in [rs(q)] + rx(q) + rz(q):
            copy.wait_send()

    staged(KR, [(0, produce), (1, pair), (3, chain), (5, finish), (5, returned)])

    def keys_done(p, carry):
        for copy in ys(p):
            copy.wait()
        return carry

    lax.fori_loop(0, KEY_PIECES, keys_done, 0)
    own_local.wait()
    own_mom.wait()


def exchange(R, F, ids, share, tokens, grads, up, down, local, momentum):
    A = MAJOR
    B = F // (2 * A)
    K = PIECES
    KR = BACK_PIECES
    D = tokens.shape[1]
    H = up.shape[1]
    T = tokens.shape[0]
    width = D // K
    wide = D // KR
    rows = F * CAP
    column = A * CAP
    half = B * column
    dma = pltpu.SemaphoreType.DMA
    vmem = pl.BlockSpec(memory_space=pltpu.VMEM)
    hbm = pl.BlockSpec(memory_space=pl.ANY)
    return pl.pallas_call(
        functools.partial(kernel, R, A, B, K, KR),
        out_shape=(
            jax.ShapeDtypeStruct((CAP, D), jnp.bfloat16),
            jax.ShapeDtypeStruct((T, T), jnp.bfloat16),
            jax.ShapeDtypeStruct((R,) + local.shape, jnp.float32),
            jax.ShapeDtypeStruct((R,) + momentum.shape, jnp.float32),
        ),
        in_specs=[vmem, vmem, hbm, hbm, hbm, hbm, hbm, hbm],
        out_specs=(vmem, vmem, hbm, hbm),
        scratch_shapes=[
            pltpu.VMEM((2 * K, T, width), jnp.bfloat16),
            pltpu.VMEM((2 * K, rows, width), jnp.bfloat16),
            pltpu.VMEM((D, H), jnp.bfloat16),
            pltpu.VMEM((K, H, width), jnp.bfloat16),
            pltpu.VMEM((CAP, T), jnp.bfloat16),
            pltpu.VMEM((CAP, 128), jnp.float32),
            pltpu.VMEM((rows, H), jnp.float32),
            pltpu.VMEM((rows, H), jnp.float32),
            pltpu.VMEM((rows, H), jnp.bfloat16),
            pltpu.VMEM((KR, rows, wide), jnp.float32),
            pltpu.VMEM((KR, half, wide), jnp.bfloat16),
            pltpu.VMEM((KR, half, wide), jnp.bfloat16),
            pltpu.VMEM((KR, B - 1, column, wide), jnp.bfloat16),
            pltpu.VMEM((KR, B - 1, column, wide), jnp.bfloat16),
            pltpu.VMEM((KR, A - 1, CAP, wide), jnp.bfloat16),
            pltpu.VMEM((KR, A - 1, CAP, wide), jnp.bfloat16),
            dma((2 * K,)),
            dma((K,)),
            dma((K,)),
            dma((2,)),
            dma((KEY_PIECES, R - 1, 2)),
            dma((KEY_PIECES, R - 1, 2)),
            dma((2 * K, A - 1)),
            dma((2 * K, A - 1)),
            dma((2 * K, B - 1)),
            dma((2 * K, B - 1)),
            dma((2 * K, B)),
            dma((2 * K, B)),
            dma((KR,)),
            dma((KR,)),
            dma((KR, B - 1)),
            dma((KR, B - 1)),
            dma((KR, A - 1)),
            dma((KR, A - 1)),
        ],
        compiler_params=pltpu.CompilerParams(
            collective_id=0, has_side_effects=True, vmem_limit_bytes=60 * 1024 * 1024
        ),
        cost_estimate=pl.CostEstimate(
            flops=6 * rows * D * H, bytes_accessed=8 * D * H, transcendentals=rows * H
        ),
    )(ids, share, tokens, grads, up, down, local, momentum)


def tail_kernel(
    R, sel_ref, res_ref, outer_ref, local_ref, mom_ref, grad_ref, new_ref, moved_ref, copy_ref
):
    r = lax.axis_index("replica")
    width = mom_ref.shape[-1]
    grad_ref[...] = dot_nn(sel_ref[:, :CAP], res_ref[...]).astype(jnp.bfloat16)
    for one in range(R):
        cols = slice(one * width, (one + 1) * width)
        outer = outer_ref[:, cols]
        pseudo = outer - local_ref[0, :, cols]
        for other in range(1, R):
            pseudo = pseudo + (outer - local_ref[other, :, cols])
        pseudo = pseudo / R
        moved = outer_beta * mom_ref[one] + pseudo
        new_outer = outer - outer_rate * (pseudo + outer_beta * moved)
        new_ref[:, cols] = new_outer
        copy_ref[:, cols] = new_outer.astype(jnp.bfloat16)

        @pl.when(r == one)
        def _():
            moved_ref[...] = moved


def tail(R, sel, result, outer, local_all, mom_all):
    T = sel.shape[0]
    D = result.shape[1]
    rows, keys = outer.shape
    width = mom_all.shape[2]
    G = TAIL_STEPS
    few, cols = rows // G, D // G
    return pl.pallas_call(
        functools.partial(tail_kernel, R),
        grid=(G,),
        out_shape=(
            jax.ShapeDtypeStruct((T, D), jnp.bfloat16),
            jax.ShapeDtypeStruct((rows, keys), jnp.float32),
            jax.ShapeDtypeStruct((rows, width), jnp.float32),
            jax.ShapeDtypeStruct((rows, keys), jnp.bfloat16),
        ),
        in_specs=[
            pl.BlockSpec((T, T), lambda g: (0, 0)),
            pl.BlockSpec((CAP, cols), lambda g: (0, g)),
            pl.BlockSpec((few, keys), lambda g: (g, 0)),
            pl.BlockSpec((R, few, keys), lambda g: (0, g, 0)),
            pl.BlockSpec((R, few, width), lambda g: (0, g, 0)),
        ],
        out_specs=(
            pl.BlockSpec((T, cols), lambda g: (0, g)),
            pl.BlockSpec((few, keys), lambda g: (g, 0)),
            pl.BlockSpec((few, width), lambda g: (g, 0)),
            pl.BlockSpec((few, keys), lambda g: (g, 0)),
        ),
        compiler_params=pltpu.CompilerParams(vmem_limit_bytes=60 * 1024 * 1024),
    )(sel, result, outer, local_all, mom_all)


def per_device(
    R,
    F,
    tokens,
    grad_out,
    expert_ids,
    gate_share,
    up_weight,
    down_weight,
    local_keys,
    outer_keys,
    momentum,
):
    result, sel, local_all, mom_all = exchange(
        R,
        F,
        expert_ids[0].T,
        gate_share,
        tokens[0],
        grad_out[0],
        up_weight[0],
        down_weight[0],
        local_keys[0],
        momentum,
    )
    input_grad, new_outer, new_momentum, outer_copy = tail(
        R, sel, result, outer_keys, local_all, mom_all
    )
    return (input_grad[None], new_outer, new_momentum, outer_copy)


def solution(mesh):
    placed = (
        P("replica", "fsdp", None),
        P("replica", "fsdp", None),
        P("replica", "fsdp", None),
        P("replica", "fsdp"),
        P("replica", None, "fsdp"),
        P("replica", "fsdp", None),
        P("replica", "fsdp", None),
        P("fsdp", None),
        P("fsdp", "replica"),
    )
    return jax.shard_map(
        functools.partial(per_device, mesh.shape["replica"], mesh.shape["fsdp"]),
        mesh=mesh,
        in_specs=placed,
        out_specs=(
            P("replica", "fsdp", None),
            P("fsdp", None),
            P("fsdp", "replica"),
            P("fsdp", None),
        ),
        check_vma=False,
    )
```

```python
import functools

import jax
import jax.numpy as jnp
from jax import lax
from jax.experimental import pallas as pl
from jax.experimental.pallas import tpu as pltpu
from jax.sharding import PartitionSpec as P

CAP = 16
MAJOR = 4
PIECES = 8
BACK_PIECES = 8
KEY_ROWS = 24
TAIL_STEPS = 8

outer_beta = 0.9
outer_rate = 0.7

MESH = pl.DeviceIdType.MESH


def dot_nn(left, right):
    return jnp.dot(left, right, preferred_element_type=jnp.float32)


def dot_nt(left, right):
    return lax.dot_general(
        left, right, (((1,), (1,)), ((), ())), preferred_element_type=jnp.float32
    )


def staged(count, stages):
    def step(t, carry):
        for lag, stage in stages:
            piece = t - lag

            @pl.when((piece >= 0) & (piece < count))
            def _():
                stage(piece)

        return carry

    lax.fori_loop(0, count + max(lag for lag, _ in stages), step, 0)


def kernel(
    R,
    A,
    B,
    K,
    KR,
    ids_ref,
    share_ref,
    tok_ref,
    grad_ref,
    up_ref,
    down_ref,
    local_ref,
    mom_ref,
    res_ref,
    sel_out_ref,
    local_all,
    mom_all,
    src,
    buf,
    upv,
    downv,
    sel_ref,
    coef_ref,
    pre_ref,
    back_ref,
    hid_ref,
    part,
    sib_out,
    sib_in,
    x_out,
    x_in,
    z_out,
    z_in,
    src_sem,
    up_sem,
    down_sem,
    own_sem,
    y_send,
    y_recv,
    gz_send,
    gz_recv,
    gx_send,
    gx_recv,
    gs_send,
    gs_recv,
    rs_send,
    rs_recv,
    rx_send,
    rx_recv,
    rz_send,
    rz_recv,
):
    r = lax.axis_index("replica")
    me = lax.axis_index("fsdp")
    c = lax.rem(me, 2)
    b = lax.rem(me // 2, B)
    a = me // (2 * B)
    NP = 2 * K
    width = src.shape[-1]
    column = A * CAP
    half = B * column

    def at(a_, b_, c_):
        return (r, (a_ * B + b_) * 2 + c_)

    sibling = at(a, b, 1 - c)
    z_peers = [at(lax.rem(a + j, A), b, c) for j in range(1, A)]
    x_peers = [at(a, lax.rem(b + j, B), c) for j in range(1, B)]
    y_peers = [(lax.rem(r + j, R), me) for j in range(1, R)]

    for k in range(K):
        cols = pl.ds(k * width, width)
        pltpu.make_async_copy(tok_ref.at[:, cols], src.at[k], src_sem.at[k]).start()
    for k in range(K):
        cols = pl.ds(k * width, width)
        pltpu.make_async_copy(up_ref.at[cols], upv.at[cols], up_sem.at[k]).start()
    for k in range(K):
        cols = pl.ds(k * width, width)
        pltpu.make_async_copy(grad_ref.at[:, cols], src.at[K + k], src_sem.at[K + k]).start()
    for k in range(K):
        cols = pl.ds(k * width, width)
        pltpu.make_async_copy(down_ref.at[:, cols], downv.at[k], down_sem.at[k]).start()
    own_local = pltpu.make_async_copy(local_ref, local_all.at[r], own_sem.at[0])
    own_mom = pltpu.make_async_copy(mom_ref, mom_all.at[r], own_sem.at[1])
    own_local.start()
    own_mom.start()

    barrier = pltpu.get_barrier_semaphore()
    peers = [sibling] + z_peers + x_peers + y_peers
    for peer in peers:
        pl.semaphore_signal(barrier, inc=1, device_id=peer, device_id_type=MESH)

    T = ids_ref.shape[1]
    first = (ids_ref[0:1, :] == 0).astype(jnp.float32)
    second = (ids_ref[1:2, :] == 0).astype(jnp.float32)
    named = jnp.broadcast_to(first + second, (T, T)).T
    row = lax.broadcasted_iota(jnp.int32, (T, T), 0)
    col = lax.broadcasted_iota(jnp.int32, (T, T), 1)
    below = jnp.where(col < row, 1.0, 0.0).astype(jnp.bfloat16)
    rank = dot_nn(below, named.astype(jnp.bfloat16))
    sel_t = jnp.where((rank == col.astype(jnp.float32)) & (named > 0.5), 1.0, 0.0)
    sel_out_ref[...] = sel_t.astype(jnp.bfloat16)
    sel = sel_t.T
    sel_ref[...] = sel[:CAP].astype(jnp.bfloat16)
    share = share_ref[...]
    coef = jnp.where(first > 0.5, share, 1.0 - share)
    coef_ref[...] = jnp.broadcast_to(
        jnp.sum(sel[:CAP] * coef, axis=1, keepdims=True), coef_ref.shape
    )
    pre_ref[...] = jnp.zeros_like(pre_ref)
    back_ref[...] = jnp.zeros_like(back_ref)

    pl.semaphore_wait(barrier, len(peers))

    def remote(source, target, send, recv, peer):
        return pltpu.make_async_remote_copy(
            src_ref=source,
            dst_ref=target,
            send_sem=send,
            recv_sem=recv,
            device_id=peer,
            device_id_type=MESH,
        )

    def rows_of(b_):
        return pl.ds(pl.multiple_of((c * B + b_) * column, column), column)

    def gz(p):
        mine = buf.at[p, pl.ds(pl.multiple_of((c * B + b) * column + a * CAP, CAP), CAP)]
        return [
            remote(mine, mine, gz_send.at[p, j], gz_recv.at[p, j], z_peers[j])
            for j in range(A - 1)
        ]

    def gx(p):
        mine = buf.at[p, rows_of(b)]
        return [
            remote(mine, mine, gx_send.at[p, j], gx_recv.at[p, j], x_peers[j])
            for j in range(B - 1)
        ]

    def gs(p, j):
        part_of = buf.at[p, rows_of(lax.rem(b + j, B))]
        return remote(part_of, part_of, gs_send.at[p, j], gs_recv.at[p, j], sibling)

    key_pieces = local_ref.shape[0] // KEY_ROWS

    def ys(p):
        rows = pl.ds(pl.multiple_of(p * KEY_ROWS, 8), KEY_ROWS)
        copies = []
        for j in range(R - 1):
            copies.append(
                remote(local_ref.at[rows], local_all.at[r, rows], y_send.at[p, j, 0], y_recv.at[p, j, 0], y_peers[j])
            )
            copies.append(
                remote(mom_ref.at[rows], mom_all.at[r, rows], y_send.at[p, j, 1], y_recv.at[p, j, 1], y_peers[j])
            )
        return copies

    def pick(p):
        pltpu.make_async_copy(tok_ref.at[:, pl.ds(0, width)], src.at[p], src_sem.at[p]).wait()
        rows = pl.ds(pl.multiple_of((c * B + b) * column + a * CAP, CAP), CAP)
        buf[p, rows, :] = dot_nn(sel_ref[...], src[p]).astype(jnp.bfloat16)
        for copy in gz(p):
            copy.start()

    def keys(p):
        @pl.when(p < key_pieces)
        def _():
            for copy in ys(p):
                copy.start()

    def across(p):
        for copy in gz(p):
            copy.wait_recv()
        for copy in gx(p):
            copy.start()
        gs(p, 0).start()

    def aside(p):
        for j, copy in enumerate(gx(p)):
            copy.wait_recv()
            gs(p, B - 1 - j).start()

    def multiply(p):
        for j in range(B):
            gs(p, j).wait_recv()

        @pl.when(p < K)
        def _():
            rows = pl.ds(pl.multiple_of(p * width, width), width)
            pltpu.make_async_copy(up_ref.at[pl.ds(0, width)], upv.at[rows], up_sem.at[p]).wait()
            pre_ref[...] += dot_nn(buf[p], upv[rows, :])

        @pl.when(p >= K)
        def _():
            k = p - K
            pltpu.make_async_copy(
                down_ref.at[:, pl.ds(0, width)], downv.at[k], down_sem.at[k]
            ).wait()
            back_ref[...] += dot_nt(buf[p], downv[k])

    def sent(p):
        for copy in gz(p) + gx(p) + [gs(p, j) for j in range(B)]:
            copy.wait_send()

    staged(NP, [(0, pick), (4, across), (7, aside), (6, keys), (9, multiply), (10, sent)])

    pre = pre_ref[...]
    sig = jax.nn.sigmoid(pre)
    hid_ref[...] = (back_ref[...] * sig * (1.0 + pre * (1.0 - sig))).astype(jnp.bfloat16)

    wide = part.shape[-1]
    own_half = pl.ds(pl.multiple_of(c * half, half), half)
    other_half = pl.ds(pl.multiple_of((1 - c) * half, half), half)

    def rs(q):
        return remote(sib_out.at[q], sib_in.at[q], rs_send.at[q], rs_recv.at[q], sibling)

    def rx(q):
        return [
            remote(x_out.at[q, j], x_in.at[q, j], rx_send.at[q, j], rx_recv.at[q, j], x_peers[j])
            for j in range(B - 1)
        ]

    def rz(q):
        return [
            remote(z_out.at[q, j], z_in.at[q, j], rz_send.at[q, j], rz_recv.at[q, j], z_peers[j])
            for j in range(A - 1)
        ]

    def produce(q):
        rows = pl.ds(pl.multiple_of(q * wide, wide), wide)
        part[q] = dot_nt(hid_ref[...], upv[rows, :])
        sib_out[q] = part[q, other_half, :].astype(jnp.bfloat16)
        rs(q).start()

    def pair(q):
        rs(q).wait_recv()
        for j, copy in enumerate(rx(q)):
            b_ = lax.rem(b + j + 1, B)
            there = pl.ds(pl.multiple_of(b_ * column, column), column)
            mine = part[q, pl.ds(pl.multiple_of(c * half + b_ * column, column), column), :]
            x_out[q, j] = (mine + sib_in[q, there, :].astype(jnp.float32)).astype(jnp.bfloat16)
            copy.start()

    def chain(q):
        here = pl.ds(pl.multiple_of(b * column, column), column)
        mine = pl.ds(pl.multiple_of(c * half + b * column, column), column)
        total = part[q, mine, :] + sib_in[q, here, :].astype(jnp.float32)
        for j, copy in enumerate(rx(q)):
            copy.wait_recv()
            total = total + x_in[q, j].astype(jnp.float32)
        part[q, mine, :] = total
        for j, copy in enumerate(rz(q)):
            a_ = lax.rem(a + j + 1, A)
            rows = pl.ds(pl.multiple_of(c * half + b * column + a_ * CAP, CAP), CAP)
            z_out[q, j] = part[q, rows, :].astype(jnp.bfloat16)
            copy.start()

    def finish(q):
        rows = pl.ds(pl.multiple_of(c * half + b * column + a * CAP, CAP), CAP)
        total = part[q, rows, :]
        for j, copy in enumerate(rz(q)):
            copy.wait_recv()
            total = total + z_in[q, j].astype(jnp.float32)
        cols = pl.ds(pl.multiple_of(q * wide, 128), wide)
        res_ref[:, cols] = (coef_ref[:, 0:1] * total).astype(jnp.bfloat16)

    def returned(q):
        for copy in [rs(q)] + rx(q) + rz(q):
            copy.wait_send()

    staged(KR, [(0, produce), (2, pair), (5, chain), (8, finish), (8, returned)])

    def keys_done(p, carry):
        for copy in ys(p):
            copy.wait()
        return carry

    lax.fori_loop(0, key_pieces, keys_done, 0)
    own_local.wait()
    own_mom.wait()


def exchange(R, F, ids, share, tokens, grads, up, down, local, momentum):
    A = MAJOR
    B = F // (2 * A)
    K = PIECES
    KR = BACK_PIECES
    D = tokens.shape[1]
    H = up.shape[1]
    T = tokens.shape[0]
    width = D // K
    wide = D // KR
    rows = F * CAP
    column = A * CAP
    half = B * column
    dma = pltpu.SemaphoreType.DMA
    vmem = pl.BlockSpec(memory_space=pltpu.VMEM)
    hbm = pl.BlockSpec(memory_space=pl.ANY)
    return pl.pallas_call(
        functools.partial(kernel, R, A, B, K, KR),
        out_shape=(
            jax.ShapeDtypeStruct((CAP, D), jnp.bfloat16),
            jax.ShapeDtypeStruct((T, T), jnp.bfloat16),
            jax.ShapeDtypeStruct((R,) + local.shape, jnp.float32),
            jax.ShapeDtypeStruct((R,) + momentum.shape, jnp.float32),
        ),
        in_specs=[vmem, vmem, hbm, hbm, hbm, hbm, hbm, hbm],
        out_specs=(vmem, vmem, hbm, hbm),
        scratch_shapes=[
            pltpu.VMEM((2 * K, T, width), jnp.bfloat16),
            pltpu.VMEM((2 * K, rows, width), jnp.bfloat16),
            pltpu.VMEM((D, H), jnp.bfloat16),
            pltpu.VMEM((K, H, width), jnp.bfloat16),
            pltpu.VMEM((CAP, T), jnp.bfloat16),
            pltpu.VMEM((CAP, 128), jnp.float32),
            pltpu.VMEM((rows, H), jnp.float32),
            pltpu.VMEM((rows, H), jnp.float32),
            pltpu.VMEM((rows, H), jnp.bfloat16),
            pltpu.VMEM((KR, rows, wide), jnp.float32),
            pltpu.VMEM((KR, half, wide), jnp.bfloat16),
            pltpu.VMEM((KR, half, wide), jnp.bfloat16),
            pltpu.VMEM((KR, B - 1, column, wide), jnp.bfloat16),
            pltpu.VMEM((KR, B - 1, column, wide), jnp.bfloat16),
            pltpu.VMEM((KR, A - 1, CAP, wide), jnp.bfloat16),
            pltpu.VMEM((KR, A - 1, CAP, wide), jnp.bfloat16),
            dma((2 * K,)),
            dma((K,)),
            dma((K,)),
            dma((2,)),
            dma((local.shape[0] // KEY_ROWS, R - 1, 2)),
            dma((local.shape[0] // KEY_ROWS, R - 1, 2)),
            dma((2 * K, A - 1)),
            dma((2 * K, A - 1)),
            dma((2 * K, B - 1)),
            dma((2 * K, B - 1)),
            dma((2 * K, B)),
            dma((2 * K, B)),
            dma((KR,)),
            dma((KR,)),
            dma((KR, B - 1)),
            dma((KR, B - 1)),
            dma((KR, A - 1)),
            dma((KR, A - 1)),
        ],
        compiler_params=pltpu.CompilerParams(
            collective_id=0, has_side_effects=True, vmem_limit_bytes=60 * 1024 * 1024
        ),
        cost_estimate=pl.CostEstimate(
            flops=6 * rows * D * H, bytes_accessed=8 * D * H, transcendentals=rows * H
        ),
    )(ids, share, tokens, grads, up, down, local, momentum)


def tail_kernel(
    R, sel_ref, res_ref, outer_ref, local_ref, mom_ref, grad_ref, new_ref, moved_ref, copy_ref
):
    r = lax.axis_index("replica")
    width = mom_ref.shape[-1]
    grad_ref[...] = dot_nn(sel_ref[:, :CAP], res_ref[...]).astype(jnp.bfloat16)
    for one in range(R):
        cols = slice(one * width, (one + 1) * width)
        outer = outer_ref[:, cols]
        pseudo = outer - local_ref[0, :, cols]
        for other in range(1, R):
            pseudo = pseudo + (outer - local_ref[other, :, cols])
        pseudo = pseudo / R
        moved = outer_beta * mom_ref[one] + pseudo
        new_outer = outer - outer_rate * (pseudo + outer_beta * moved)
        new_ref[:, cols] = new_outer
        copy_ref[:, cols] = new_outer.astype(jnp.bfloat16)

        @pl.when(r == one)
        def _():
            moved_ref[...] = moved


def tail(R, sel, result, outer, local_all, mom_all):
    T = sel.shape[0]
    D = result.shape[1]
    rows, keys = outer.shape
    width = mom_all.shape[2]
    G = TAIL_STEPS
    few, cols = rows // G, D // G
    return pl.pallas_call(
        functools.partial(tail_kernel, R),
        grid=(G,),
        out_shape=(
            jax.ShapeDtypeStruct((T, D), jnp.bfloat16),
            jax.ShapeDtypeStruct((rows, keys), jnp.float32),
            jax.ShapeDtypeStruct((rows, width), jnp.float32),
            jax.ShapeDtypeStruct((rows, keys), jnp.bfloat16),
        ),
        in_specs=[
            pl.BlockSpec((T, T), lambda g: (0, 0)),
            pl.BlockSpec((CAP, cols), lambda g: (0, g)),
            pl.BlockSpec((few, keys), lambda g: (g, 0)),
            pl.BlockSpec((R, few, keys), lambda g: (0, g, 0)),
            pl.BlockSpec((R, few, width), lambda g: (0, g, 0)),
        ],
        out_specs=(
            pl.BlockSpec((T, cols), lambda g: (0, g)),
            pl.BlockSpec((few, keys), lambda g: (g, 0)),
            pl.BlockSpec((few, width), lambda g: (g, 0)),
            pl.BlockSpec((few, keys), lambda g: (g, 0)),
        ),
        compiler_params=pltpu.CompilerParams(vmem_limit_bytes=60 * 1024 * 1024),
    )(sel, result, outer, local_all, mom_all)


def per_device(
    R,
    F,
    tokens,
    grad_out,
    expert_ids,
    gate_share,
    up_weight,
    down_weight,
    local_keys,
    outer_keys,
    momentum,
):
    result, sel, local_all, mom_all = exchange(
        R,
        F,
        expert_ids[0].T,
        gate_share,
        tokens[0],
        grad_out[0],
        up_weight[0],
        down_weight[0],
        local_keys[0],
        momentum,
    )
    input_grad, new_outer, new_momentum, outer_copy = tail(
        R, sel, result, outer_keys, local_all, mom_all
    )
    return (input_grad[None], new_outer, new_momentum, outer_copy)


def solution(mesh):
    placed = (
        P("replica", "fsdp", None),
        P("replica", "fsdp", None),
        P("replica", "fsdp", None),
        P("replica", "fsdp"),
        P("replica", None, "fsdp"),
        P("replica", "fsdp", None),
        P("replica", "fsdp", None),
        P("fsdp", None),
        P("fsdp", "replica"),
    )
    return jax.shard_map(
        functools.partial(per_device, mesh.shape["replica"], mesh.shape["fsdp"]),
        mesh=mesh,
        in_specs=placed,
        out_specs=(
            P("replica", "fsdp", None),
            P("fsdp", None),
            P("fsdp", "replica"),
            P("fsdp", None),
        ),
        check_vma=False,
    )
```

```python
import functools

import jax
import jax.numpy as jnp
from jax import lax
from jax.experimental import pallas as pl
from jax.experimental.pallas import tpu as pltpu
from jax.sharding import PartitionSpec as P

CAP = 16
MAJOR = 4
PIECES = 8
BACK_PIECES = 8
KEY_ROWS = 48
TAIL_STEPS = 2

outer_beta = 0.9
outer_rate = 0.7

MESH = pl.DeviceIdType.MESH


def dot_nn(left, right):
    return jnp.dot(left, right, preferred_element_type=jnp.float32)


def dot_nt(left, right):
    return lax.dot_general(
        left, right, (((1,), (1,)), ((), ())), preferred_element_type=jnp.float32
    )


def staged(count, stages):
    def step(t, carry):
        for lag, stage in stages:
            piece = t - lag

            @pl.when((piece >= 0) & (piece < count))
            def _():
                stage(piece)

        return carry

    lax.fori_loop(0, count + max(lag for lag, _ in stages), step, 0)


def kernel(
    R,
    A,
    B,
    K,
    KR,
    ids_ref,
    share_ref,
    tok_ref,
    grad_ref,
    up_ref,
    down_ref,
    local_ref,
    mom_ref,
    res_ref,
    sel_out_ref,
    local_all,
    mom_all,
    src,
    buf,
    upv,
    downv,
    sel_ref,
    coef_ref,
    pre_ref,
    back_ref,
    hid_ref,
    part,
    sib_out,
    sib_in,
    x_out,
    x_in,
    z_out,
    z_in,
    src_sem,
    up_sem,
    down_sem,
    own_sem,
    y_send,
    y_recv,
    gz_send,
    gz_recv,
    go_send,
    go_recv,
    gx_send,
    gx_recv,
    gs_send,
    gs_recv,
    rs_send,
    rs_recv,
    rx_send,
    rx_recv,
    rz_send,
    rz_recv,
):
    r = lax.axis_index("replica")
    me = lax.axis_index("fsdp")
    c = lax.rem(me, 2)
    b = lax.rem(me // 2, B)
    a = me // (2 * B)
    NP = 2 * K
    width = src.shape[-1]
    column = A * CAP
    half = B * column

    def at(a_, b_, c_):
        return (r, (a_ * B + b_) * 2 + c_)

    sibling = at(a, b, 1 - c)
    z_peers = [at(lax.rem(a + j, A), b, c) for j in range(1, A)]
    x_peers = [at(a, lax.rem(b + j, B), c) for j in range(1, B)]
    y_peers = [(lax.rem(r + j, R), me) for j in range(1, R)]

    for k in range(K):
        cols = pl.ds(k * width, width)
        pltpu.make_async_copy(tok_ref.at[:, cols], src.at[k], src_sem.at[k]).start()
    for k in range(K):
        cols = pl.ds(k * width, width)
        pltpu.make_async_copy(up_ref.at[cols], upv.at[cols], up_sem.at[k]).start()
    for k in range(K):
        cols = pl.ds(k * width, width)
        pltpu.make_async_copy(grad_ref.at[:, cols], src.at[K + k], src_sem.at[K + k]).start()
    for k in range(K):
        cols = pl.ds(k * width, width)
        pltpu.make_async_copy(down_ref.at[:, cols], downv.at[k], down_sem.at[k]).start()
    own_local = pltpu.make_async_copy(local_ref, local_all.at[r], own_sem.at[0])
    own_mom = pltpu.make_async_copy(mom_ref, mom_all.at[r], own_sem.at[1])
    own_local.start()
    own_mom.start()

    barrier = pltpu.get_barrier_semaphore()
    peers = [sibling] + z_peers + x_peers + y_peers
    for peer in peers:
        pl.semaphore_signal(barrier, inc=1, device_id=peer, device_id_type=MESH)

    T = ids_ref.shape[1]
    first = (ids_ref[0:1, :] == 0).astype(jnp.float32)
    second = (ids_ref[1:2, :] == 0).astype(jnp.float32)
    named = jnp.broadcast_to(first + second, (T, T)).T
    row = lax.broadcasted_iota(jnp.int32, (T, T), 0)
    col = lax.broadcasted_iota(jnp.int32, (T, T), 1)
    below = jnp.where(col < row, 1.0, 0.0).astype(jnp.bfloat16)
    rank = dot_nn(below, named.astype(jnp.bfloat16))
    sel_t = jnp.where((rank == col.astype(jnp.float32)) & (named > 0.5), 1.0, 0.0)
    sel_out_ref[...] = sel_t.astype(jnp.bfloat16)
    sel = sel_t.T
    sel_ref[...] = sel[:CAP].astype(jnp.bfloat16)
    share = share_ref[...]
    coef = jnp.where(first > 0.5, share, 1.0 - share)
    coef_ref[...] = jnp.broadcast_to(
        jnp.sum(sel[:CAP] * coef, axis=1, keepdims=True), coef_ref.shape
    )
    pre_ref[...] = jnp.zeros_like(pre_ref)
    back_ref[...] = jnp.zeros_like(back_ref)

    pl.semaphore_wait(barrier, len(peers))

    def remote(source, target, send, recv, peer):
        return pltpu.make_async_remote_copy(
            src_ref=source,
            dst_ref=target,
            send_sem=send,
            recv_sem=recv,
            device_id=peer,
            device_id_type=MESH,
        )

    def rows_of(b_):
        return pl.ds(pl.multiple_of((c * B + b_) * column, column), column)

    def place(b_, k):
        return pl.ds(pl.multiple_of((c * B + b_) * column + k * CAP, CAP), CAP)

    def gz(p):
        return [
            remote(buf.at[p, place(b, 0)], buf.at[p, place(b, A - 1 - j)], gz_send.at[p, j], gz_recv.at[p, j], z_peers[j])
            for j in range(A - 1)
        ]

    def gx_own(p):
        mine = buf.at[p, place(b, 0)]
        return [
            remote(mine, mine, go_send.at[p, j], go_recv.at[p, j], x_peers[j])
            for j in range(B - 1)
        ]

    def gx(p):
        rows = pl.ds(pl.multiple_of((c * B + b) * column + CAP, CAP), column - CAP)
        rest = buf.at[p, rows]
        return [
            remote(rest, rest, gx_send.at[p, j], gx_recv.at[p, j], x_peers[j])
            for j in range(B - 1)
        ]

    def gs(p, j):
        part_of = buf.at[p, rows_of(lax.rem(b + j, B))]
        return remote(part_of, part_of, gs_send.at[p, j], gs_recv.at[p, j], sibling)

    key_pieces = local_ref.shape[0] // KEY_ROWS

    def ys(p):
        rows = pl.ds(pl.multiple_of(p * KEY_ROWS, 8), KEY_ROWS)
        copies = []
        for j in range(R - 1):
            copies.append(
                remote(local_ref.at[rows], local_all.at[r, rows], y_send.at[p, j, 0], y_recv.at[p, j, 0], y_peers[j])
            )
            copies.append(
                remote(mom_ref.at[rows], mom_all.at[r, rows], y_send.at[p, j, 1], y_recv.at[p, j, 1], y_peers[j])
            )
        return copies

    def pick(p):
        pltpu.make_async_copy(tok_ref.at[:, pl.ds(0, width)], src.at[p], src_sem.at[p]).wait()
        buf[p, place(b, 0), :] = dot_nn(sel_ref[...], src[p]).astype(jnp.bfloat16)
        for copy in gx_own(p) + gz(p):
            copy.start()

    def keys(p):
        @pl.when(p < key_pieces)
        def _():
            for copy in ys(p):
                copy.start()

    def across(p):
        for copy in gz(p):
            copy.wait_recv()
        for copy in gx(p):
            copy.start()
        gs(p, 0).start()

    def aside(p):
        for j in range(B - 1):
            gx_own(p)[j].wait_recv()
            gx(p)[j].wait_recv()
            gs(p, B - 1 - j).start()

    def multiply(p):
        for j in range(B):
            gs(p, j).wait_recv()

        @pl.when(p < K)
        def _():
            rows = pl.ds(pl.multiple_of(p * width, width), width)
            pltpu.make_async_copy(up_ref.at[pl.ds(0, width)], upv.at[rows], up_sem.at[p]).wait()
            pre_ref[...] += dot_nn(buf[p], upv[rows, :])

        @pl.when(p >= K)
        def _():
            k = p - K
            pltpu.make_async_copy(
                down_ref.at[:, pl.ds(0, width)], downv.at[k], down_sem.at[k]
            ).wait()
            back_ref[...] += dot_nt(buf[p], downv[k])

    def sent(p):
        for copy in gz(p) + gx_own(p) + gx(p) + [gs(p, j) for j in range(B)]:
            copy.wait_send()

    staged(NP, [(0, pick), (2, across), (2, keys), (4, aside), (6, multiply), (7, sent)])

    pre = pre_ref[...]
    sig = jax.nn.sigmoid(pre)
    hid_ref[...] = (back_ref[...] * sig * (1.0 + pre * (1.0 - sig))).astype(jnp.bfloat16)

    wide = part.shape[-1]
    own_half = pl.ds(pl.multiple_of(c * half, half), half)
    other_half = pl.ds(pl.multiple_of((1 - c) * half, half), half)

    def rs(q):
        return remote(sib_out.at[q], sib_in.at[q], rs_send.at[q], rs_recv.at[q], sibling)

    def rx(q):
        return [
            remote(x_out.at[q, j], x_in.at[q, j], rx_send.at[q, j], rx_recv.at[q, j], x_peers[j])
            for j in range(B - 1)
        ]

    def rz(q):
        return [
            remote(z_out.at[q, j], z_in.at[q, j], rz_send.at[q, j], rz_recv.at[q, j], z_peers[j])
            for j in range(A - 1)
        ]

    def produce(q):
        rows = pl.ds(pl.multiple_of(q * wide, wide), wide)
        part[q] = dot_nt(hid_ref[...], upv[rows, :])
        sib_out[q] = part[q, other_half, :].astype(jnp.bfloat16)
        rs(q).start()

    def pair(q):
        rs(q).wait_recv()
        for j, copy in enumerate(rx(q)):
            b_ = lax.rem(b + j + 1, B)
            there = pl.ds(pl.multiple_of(b_ * column, column), column)
            mine = part[q, pl.ds(pl.multiple_of(c * half + b_ * column, column), column), :]
            x_out[q, j] = (mine + sib_in[q, there, :].astype(jnp.float32)).astype(jnp.bfloat16)
            copy.start()

    def chain(q):
        here = pl.ds(pl.multiple_of(b * column, column), column)
        mine = pl.ds(pl.multiple_of(c * half + b * column, column), column)
        total = part[q, mine, :] + sib_in[q, here, :].astype(jnp.float32)
        for j, copy in enumerate(rx(q)):
            copy.wait_recv()
            total = total + x_in[q, j].astype(jnp.float32)
        part[q, mine, :] = total
        for j, copy in enumerate(rz(q)):
            z_out[q, j] = part[q, place(b, j + 1), :].astype(jnp.bfloat16)
            copy.start()

    def finish(q):
        total = part[q, place(b, 0), :]
        for j, copy in enumerate(rz(q)):
            copy.wait_recv()
            total = total + z_in[q, j].astype(jnp.float32)
        cols = pl.ds(pl.multiple_of(q * wide, 128), wide)
        res_ref[:, cols] = (coef_ref[:, 0:1] * total).astype(jnp.bfloat16)

    def returned(q):
        for copy in [rs(q)] + rx(q) + rz(q):
            copy.wait_send()

    staged(KR, [(0, produce), (1, pair), (3, chain), (5, finish), (6, returned)])

    def keys_done(p, carry):
        for copy in ys(p):
            copy.wait()
        return carry

    lax.fori_loop(0, key_pieces, keys_done, 0)
    own_local.wait()
    own_mom.wait()


def exchange(R, F, ids, share, tokens, grads, up, down, local, momentum):
    A = MAJOR
    B = F // (2 * A)
    K = PIECES
    KR = BACK_PIECES
    D = tokens.shape[1]
    H = up.shape[1]
    T = tokens.shape[0]
    width = D // K
    wide = D // KR
    rows = F * CAP
    column = A * CAP
    half = B * column
    dma = pltpu.SemaphoreType.DMA
    vmem = pl.BlockSpec(memory_space=pltpu.VMEM)
    hbm = pl.BlockSpec(memory_space=pl.ANY)
    return pl.pallas_call(
        functools.partial(kernel, R, A, B, K, KR),
        out_shape=(
            jax.ShapeDtypeStruct((CAP, D), jnp.bfloat16),
            jax.ShapeDtypeStruct((T, T), jnp.bfloat16),
            jax.ShapeDtypeStruct((R,) + local.shape, jnp.float32),
            jax.ShapeDtypeStruct((R,) + momentum.shape, jnp.float32),
        ),
        in_specs=[vmem, vmem, hbm, hbm, hbm, hbm, hbm, hbm],
        out_specs=(vmem, vmem, hbm, hbm),
        scratch_shapes=[
            pltpu.VMEM((2 * K, T, width), jnp.bfloat16),
            pltpu.VMEM((2 * K, rows, width), jnp.bfloat16),
            pltpu.VMEM((D, H), jnp.bfloat16),
            pltpu.VMEM((K, H, width), jnp.bfloat16),
            pltpu.VMEM((CAP, T), jnp.bfloat16),
            pltpu.VMEM((CAP, 128), jnp.float32),
            pltpu.VMEM((rows, H), jnp.float32),
            pltpu.VMEM((rows, H), jnp.float32),
            pltpu.VMEM((rows, H), jnp.bfloat16),
            pltpu.VMEM((KR, rows, wide), jnp.float32),
            pltpu.VMEM((KR, half, wide), jnp.bfloat16),
            pltpu.VMEM((KR, half, wide), jnp.bfloat16),
            pltpu.VMEM((KR, B - 1, column, wide), jnp.bfloat16),
            pltpu.VMEM((KR, B - 1, column, wide), jnp.bfloat16),
            pltpu.VMEM((KR, A - 1, CAP, wide), jnp.bfloat16),
            pltpu.VMEM((KR, A - 1, CAP, wide), jnp.bfloat16),
            dma((2 * K,)),
            dma((K,)),
            dma((K,)),
            dma((2,)),
            dma((local.shape[0] // KEY_ROWS, R - 1, 2)),
            dma((local.shape[0] // KEY_ROWS, R - 1, 2)),
            dma((2 * K, A - 1)),
            dma((2 * K, A - 1)),
            dma((2 * K, B - 1)),
            dma((2 * K, B - 1)),
            dma((2 * K, B - 1)),
            dma((2 * K, B - 1)),
            dma((2 * K, B)),
            dma((2 * K, B)),
            dma((KR,)),
            dma((KR,)),
            dma((KR, B - 1)),
            dma((KR, B - 1)),
            dma((KR, A - 1)),
            dma((KR, A - 1)),
        ],
        compiler_params=pltpu.CompilerParams(
            collective_id=0, has_side_effects=True, vmem_limit_bytes=60 * 1024 * 1024
        ),
        cost_estimate=pl.CostEstimate(
            flops=6 * rows * D * H, bytes_accessed=8 * D * H, transcendentals=rows * H
        ),
    )(ids, share, tokens, grads, up, down, local, momentum)


def tail_kernel(
    R, sel_ref, res_ref, outer_ref, local_ref, mom_ref, grad_ref, new_ref, moved_ref, copy_ref
):
    r = lax.axis_index("replica")
    width = mom_ref.shape[-1]
    grad_ref[...] = dot_nn(sel_ref[:, :CAP], res_ref[...]).astype(jnp.bfloat16)
    for one in range(R):
        cols = slice(one * width, (one + 1) * width)
        outer = outer_ref[:, cols]
        pseudo = outer - local_ref[0, :, cols]
        for other in range(1, R):
            pseudo = pseudo + (outer - local_ref[other, :, cols])
        pseudo = pseudo / R
        moved = outer_beta * mom_ref[one] + pseudo
        new_outer = outer - outer_rate * (pseudo + outer_beta * moved)
        new_ref[:, cols] = new_outer
        copy_ref[:, cols] = new_outer.astype(jnp.bfloat16)

        @pl.when(r == one)
        def _():
            moved_ref[...] = moved


def tail(R, sel, result, outer, local_all, mom_all):
    T = sel.shape[0]
    D = result.shape[1]
    rows, keys = outer.shape
    width = mom_all.shape[2]
    G = TAIL_STEPS
    few, cols = rows // G, D // G
    return pl.pallas_call(
        functools.partial(tail_kernel, R),
        grid=(G,),
        out_shape=(
            jax.ShapeDtypeStruct((T, D), jnp.bfloat16),
            jax.ShapeDtypeStruct((rows, keys), jnp.float32),
            jax.ShapeDtypeStruct((rows, width), jnp.float32),
            jax.ShapeDtypeStruct((rows, keys), jnp.bfloat16),
        ),
        in_specs=[
            pl.BlockSpec((T, T), lambda g: (0, 0)),
            pl.BlockSpec((CAP, cols), lambda g: (0, g)),
            pl.BlockSpec((few, keys), lambda g: (g, 0)),
            pl.BlockSpec((R, few, keys), lambda g: (0, g, 0)),
            pl.BlockSpec((R, few, width), lambda g: (0, g, 0)),
        ],
        out_specs=(
            pl.BlockSpec((T, cols), lambda g: (0, g)),
            pl.BlockSpec((few, keys), lambda g: (g, 0)),
            pl.BlockSpec((few, width), lambda g: (g, 0)),
            pl.BlockSpec((few, keys), lambda g: (g, 0)),
        ),
        compiler_params=pltpu.CompilerParams(vmem_limit_bytes=60 * 1024 * 1024),
    )(sel, result, outer, local_all, mom_all)


def per_device(
    R,
    F,
    tokens,
    grad_out,
    expert_ids,
    gate_share,
    up_weight,
    down_weight,
    local_keys,
    outer_keys,
    momentum,
):
    result, sel, local_all, mom_all = exchange(
        R,
        F,
        expert_ids[0].T,
        gate_share,
        tokens[0],
        grad_out[0],
        up_weight[0],
        down_weight[0],
        local_keys[0],
        momentum,
    )
    input_grad, new_outer, new_momentum, outer_copy = tail(
        R, sel, result, outer_keys, local_all, mom_all
    )
    return (input_grad[None], new_outer, new_momentum, outer_copy)


def solution(mesh):
    placed = (
        P("replica", "fsdp", None),
        P("replica", "fsdp", None),
        P("replica", "fsdp", None),
        P("replica", "fsdp"),
        P("replica", None, "fsdp"),
        P("replica", "fsdp", None),
        P("replica", "fsdp", None),
        P("fsdp", None),
        P("fsdp", "replica"),
    )
    return jax.shard_map(
        functools.partial(per_device, mesh.shape["replica"], mesh.shape["fsdp"]),
        mesh=mesh,
        in_specs=placed,
        out_specs=(
            P("replica", "fsdp", None),
            P("fsdp", None),
            P("fsdp", "replica"),
            P("fsdp", None),
        ),
        check_vma=False,
    )
```

```python
import functools

import jax
import jax.numpy as jnp
from jax import lax
from jax.experimental import pallas as pl
from jax.experimental.pallas import tpu as pltpu
from jax.sharding import PartitionSpec as P

CAP = 16
MAJOR = 4
PIECES = 12
BACK_PIECES = 12
KEY_ROWS = 48
TAIL_STEPS = 2

outer_beta = 0.9
outer_rate = 0.7

MESH = pl.DeviceIdType.MESH


def dot_nn(left, right):
    return jnp.dot(left, right, preferred_element_type=jnp.float32)


def dot_nt(left, right):
    return lax.dot_general(
        left, right, (((1,), (1,)), ((), ())), preferred_element_type=jnp.float32
    )


def staged(count, stages):
    def step(t, carry):
        for lag, stage in stages:
            piece = t - lag

            @pl.when((piece >= 0) & (piece < count))
            def _():
                stage(piece)

        return carry

    lax.fori_loop(0, count + max(lag for lag, _ in stages), step, 0)


def kernel(
    R,
    A,
    B,
    K,
    KR,
    ids_ref,
    share_ref,
    tok_ref,
    grad_ref,
    up_ref,
    down_ref,
    local_ref,
    mom_ref,
    res_ref,
    sel_out_ref,
    local_all,
    mom_all,
    src,
    buf,
    upv,
    downv,
    sel_ref,
    coef_ref,
    pre_ref,
    back_ref,
    hid_ref,
    part,
    sib_out,
    sib_in,
    x_out,
    x_in,
    z_out,
    z_in,
    src_sem,
    up_sem,
    down_sem,
    own_sem,
    y_send,
    y_recv,
    gz_send,
    gz_recv,
    go_send,
    go_recv,
    gx_send,
    gx_recv,
    gs_send,
    gs_recv,
    rs_send,
    rs_recv,
    rx_send,
    rx_recv,
    rz_send,
    rz_recv,
):
    r = lax.axis_index("replica")
    me = lax.axis_index("fsdp")
    c = lax.rem(me, 2)
    b = lax.rem(me // 2, B)
    a = me // (2 * B)
    NP = 2 * K
    width = src.shape[-1]
    column = A * CAP
    half = B * column

    def at(a_, b_, c_):
        return (r, (a_ * B + b_) * 2 + c_)

    sibling = at(a, b, 1 - c)
    z_peers = [at(lax.rem(a + j, A), b, c) for j in range(1, A)]
    x_peers = [at(a, lax.rem(b + j, B), c) for j in range(1, B)]
    y_peers = [(lax.rem(r + j, R), me) for j in range(1, R)]

    for k in range(K):
        cols = pl.ds(k * width, width)
        pltpu.make_async_copy(tok_ref.at[:, cols], src.at[k], src_sem.at[k]).start()
    for k in range(K):
        cols = pl.ds(k * width, width)
        pltpu.make_async_copy(up_ref.at[cols], upv.at[cols], up_sem.at[k]).start()
    for k in range(K):
        cols = pl.ds(k * width, width)
        pltpu.make_async_copy(grad_ref.at[:, cols], src.at[K + k], src_sem.at[K + k]).start()
    for k in range(K):
        cols = pl.ds(k * width, width)
        pltpu.make_async_copy(down_ref.at[:, cols], downv.at[k], down_sem.at[k]).start()
    own_local = pltpu.make_async_copy(local_ref, local_all.at[r], own_sem.at[0])
    own_mom = pltpu.make_async_copy(mom_ref, mom_all.at[r], own_sem.at[1])
    own_local.start()
    own_mom.start()

    barrier = pltpu.get_barrier_semaphore()
    peers = [sibling] + z_peers + x_peers + y_peers
    for peer in peers:
        pl.semaphore_signal(barrier, inc=1, device_id=peer, device_id_type=MESH)

    T = ids_ref.shape[1]
    first = (ids_ref[0:1, :] == 0).astype(jnp.float32)
    second = (ids_ref[1:2, :] == 0).astype(jnp.float32)
    named = jnp.broadcast_to(first + second, (T, T)).T
    row = lax.broadcasted_iota(jnp.int32, (T, T), 0)
    col = lax.broadcasted_iota(jnp.int32, (T, T), 1)
    below = jnp.where(col < row, 1.0, 0.0).astype(jnp.bfloat16)
    rank = dot_nn(below, named.astype(jnp.bfloat16))
    sel_t = jnp.where((rank == col.astype(jnp.float32)) & (named > 0.5), 1.0, 0.0)
    sel_out_ref[...] = sel_t.astype(jnp.bfloat16)
    sel = sel_t.T
    sel_ref[...] = sel[:CAP].astype(jnp.bfloat16)
    share = share_ref[...]
    coef = jnp.where(first > 0.5, share, 1.0 - share)
    coef_ref[...] = jnp.broadcast_to(
        jnp.sum(sel[:CAP] * coef, axis=1, keepdims=True), coef_ref.shape
    )
    pre_ref[...] = jnp.zeros_like(pre_ref)
    back_ref[...] = jnp.zeros_like(back_ref)

    pl.semaphore_wait(barrier, len(peers))

    def remote(source, target, send, recv, peer):
        return pltpu.make_async_remote_copy(
            src_ref=source,
            dst_ref=target,
            send_sem=send,
            recv_sem=recv,
            device_id=peer,
            device_id_type=MESH,
        )

    def rows_of(b_):
        return pl.ds(pl.multiple_of((c * B + b_) * column, column), column)

    def place(b_, k):
        return pl.ds(pl.multiple_of((c * B + b_) * column + k * CAP, CAP), CAP)

    def gz(p):
        return [
            remote(buf.at[p, place(b, 0)], buf.at[p, place(b, A - 1 - j)], gz_send.at[p, j], gz_recv.at[p, j], z_peers[j])
            for j in range(A - 1)
        ]

    def gx_own(p):
        mine = buf.at[p, place(b, 0)]
        return [
            remote(mine, mine, go_send.at[p, j], go_recv.at[p, j], x_peers[j])
            for j in range(B - 1)
        ]

    def gx(p):
        rows = pl.ds(pl.multiple_of((c * B + b) * column + CAP, CAP), column - CAP)
        rest = buf.at[p, rows]
        return [
            remote(rest, rest, gx_send.at[p, j], gx_recv.at[p, j], x_peers[j])
            for j in range(B - 1)
        ]

    def gs(p, j):
        part_of = buf.at[p, rows_of(lax.rem(b + j, B))]
        return remote(part_of, part_of, gs_send.at[p, j], gs_recv.at[p, j], sibling)

    key_pieces = local_ref.shape[0] // KEY_ROWS

    def ys(p):
        rows = pl.ds(pl.multiple_of(p * KEY_ROWS, 8), KEY_ROWS)
        copies = []
        for j in range(R - 1):
            copies.append(
                remote(local_ref.at[rows], local_all.at[r, rows], y_send.at[p, j, 0], y_recv.at[p, j, 0], y_peers[j])
            )
            copies.append(
                remote(mom_ref.at[rows], mom_all.at[r, rows], y_send.at[p, j, 1], y_recv.at[p, j, 1], y_peers[j])
            )
        return copies

    def pick(p):
        pltpu.make_async_copy(tok_ref.at[:, pl.ds(0, width)], src.at[p], src_sem.at[p]).wait()
        buf[p, place(b, 0), :] = dot_nn(sel_ref[...], src[p]).astype(jnp.bfloat16)
        for copy in gx_own(p) + gz(p):
            copy.start()

    def keys(p):
        @pl.when(p < key_pieces)
        def _():
            for copy in ys(p):
                copy.start()

    def across(p):
        for copy in gz(p):
            copy.wait_recv()
        for copy in gx(p):
            copy.start()
        gs(p, 0).start()

    def aside(p):
        for j in range(B - 1):
            gx_own(p)[j].wait_recv()
            gx(p)[j].wait_recv()
            gs(p, B - 1 - j).start()

    def multiply(p):
        for j in range(B):
            gs(p, j).wait_recv()

        @pl.when(p < K)
        def _():
            rows = pl.ds(pl.multiple_of(p * width, width), width)
            pltpu.make_async_copy(up_ref.at[pl.ds(0, width)], upv.at[rows], up_sem.at[p]).wait()
            pre_ref[...] += dot_nn(buf[p], upv[rows, :])

        @pl.when(p >= K)
        def _():
            k = p - K
            pltpu.make_async_copy(
                down_ref.at[:, pl.ds(0, width)], downv.at[k], down_sem.at[k]
            ).wait()
            back_ref[...] += dot_nt(buf[p], downv[k])

    def sent(p):
        for copy in gz(p) + gx_own(p) + gx(p) + [gs(p, j) for j in range(B)]:
            copy.wait_send()

    staged(NP, [(0, pick), (3, across), (3, keys), (5, aside), (7, multiply), (8, sent)])

    pre = pre_ref[...]
    sig = jax.nn.sigmoid(pre)
    hid_ref[...] = (back_ref[...] * sig * (1.0 + pre * (1.0 - sig))).astype(jnp.bfloat16)

    wide = part.shape[-1]
    own_half = pl.ds(pl.multiple_of(c * half, half), half)
    other_half = pl.ds(pl.multiple_of((1 - c) * half, half), half)

    def rs(q):
        return remote(sib_out.at[q], sib_in.at[q], rs_send.at[q], rs_recv.at[q], sibling)

    def rx(q):
        return [
            remote(x_out.at[q, j], x_in.at[q, j], rx_send.at[q, j], rx_recv.at[q, j], x_peers[j])
            for j in range(B - 1)
        ]

    def rz(q):
        return [
            remote(z_out.at[q, j], z_in.at[q, j], rz_send.at[q, j], rz_recv.at[q, j], z_peers[j])
            for j in range(A - 1)
        ]

    def produce(q):
        rows = pl.ds(pl.multiple_of(q * wide, wide), wide)
        part[q] = dot_nt(hid_ref[...], upv[rows, :])
        sib_out[q] = part[q, other_half, :].astype(jnp.bfloat16)
        rs(q).start()

    def pair(q):
        rs(q).wait_recv()
        for j, copy in enumerate(rx(q)):
            b_ = lax.rem(b + j + 1, B)
            there = pl.ds(pl.multiple_of(b_ * column, column), column)
            mine = part[q, pl.ds(pl.multiple_of(c * half + b_ * column, column), column), :]
            x_out[q, j] = (mine + sib_in[q, there, :].astype(jnp.float32)).astype(jnp.bfloat16)
            copy.start()

    def chain(q):
        here = pl.ds(pl.multiple_of(b * column, column), column)
        mine = pl.ds(pl.multiple_of(c * half + b * column, column), column)
        total = part[q, mine, :] + sib_in[q, here, :].astype(jnp.float32)
        for j, copy in enumerate(rx(q)):
            copy.wait_recv()
            total = total + x_in[q, j].astype(jnp.float32)
        part[q, mine, :] = total
        for j, copy in enumerate(rz(q)):
            z_out[q, j] = part[q, place(b, j + 1), :].astype(jnp.bfloat16)
            copy.start()

    def finish(q):
        total = part[q, place(b, 0), :]
        for j, copy in enumerate(rz(q)):
            copy.wait_recv()
            total = total + z_in[q, j].astype(jnp.float32)
        cols = pl.ds(pl.multiple_of(q * wide, 128), wide)
        res_ref[:, cols] = (coef_ref[:, 0:1] * total).astype(jnp.bfloat16)

    def returned(q):
        for copy in [rs(q)] + rx(q) + rz(q):
            copy.wait_send()

    staged(KR, [(0, produce), (2, pair), (5, chain), (8, finish), (9, returned)])

    def keys_done(p, carry):
        for copy in ys(p):
            copy.wait()
        return carry

    lax.fori_loop(0, key_pieces, keys_done, 0)
    own_local.wait()
    own_mom.wait()


def exchange(R, F, ids, share, tokens, grads, up, down, local, momentum):
    A = MAJOR
    B = F // (2 * A)
    K = PIECES
    KR = BACK_PIECES
    D = tokens.shape[1]
    H = up.shape[1]
    T = tokens.shape[0]
    width = D // K
    wide = D // KR
    rows = F * CAP
    column = A * CAP
    half = B * column
    dma = pltpu.SemaphoreType.DMA
    vmem = pl.BlockSpec(memory_space=pltpu.VMEM)
    hbm = pl.BlockSpec(memory_space=pl.ANY)
    return pl.pallas_call(
        functools.partial(kernel, R, A, B, K, KR),
        out_shape=(
            jax.ShapeDtypeStruct((CAP, D), jnp.bfloat16),
            jax.ShapeDtypeStruct((T, T), jnp.bfloat16),
            jax.ShapeDtypeStruct((R,) + local.shape, jnp.float32),
            jax.ShapeDtypeStruct((R,) + momentum.shape, jnp.float32),
        ),
        in_specs=[vmem, vmem, hbm, hbm, hbm, hbm, hbm, hbm],
        out_specs=(vmem, vmem, hbm, hbm),
        scratch_shapes=[
            pltpu.VMEM((2 * K, T, width), jnp.bfloat16),
            pltpu.VMEM((2 * K, rows, width), jnp.bfloat16),
            pltpu.VMEM((D, H), jnp.bfloat16),
            pltpu.VMEM((K, H, width), jnp.bfloat16),
            pltpu.VMEM((CAP, T), jnp.bfloat16),
            pltpu.VMEM((CAP, 128), jnp.float32),
            pltpu.VMEM((rows, H), jnp.float32),
            pltpu.VMEM((rows, H), jnp.float32),
            pltpu.VMEM((rows, H), jnp.bfloat16),
            pltpu.VMEM((KR, rows, wide), jnp.float32),
            pltpu.VMEM((KR, half, wide), jnp.bfloat16),
            pltpu.VMEM((KR, half, wide), jnp.bfloat16),
            pltpu.VMEM((KR, B - 1, column, wide), jnp.bfloat16),
            pltpu.VMEM((KR, B - 1, column, wide), jnp.bfloat16),
            pltpu.VMEM((KR, A - 1, CAP, wide), jnp.bfloat16),
            pltpu.VMEM((KR, A - 1, CAP, wide), jnp.bfloat16),
            dma((2 * K,)),
            dma((K,)),
            dma((K,)),
            dma((2,)),
            dma((local.shape[0] // KEY_ROWS, R - 1, 2)),
            dma((local.shape[0] // KEY_ROWS, R - 1, 2)),
            dma((2 * K, A - 1)),
            dma((2 * K, A - 1)),
            dma((2 * K, B - 1)),
            dma((2 * K, B - 1)),
            dma((2 * K, B - 1)),
            dma((2 * K, B - 1)),
            dma((2 * K, B)),
            dma((2 * K, B)),
            dma((KR,)),
            dma((KR,)),
            dma((KR, B - 1)),
            dma((KR, B - 1)),
            dma((KR, A - 1)),
            dma((KR, A - 1)),
        ],
        compiler_params=pltpu.CompilerParams(
            collective_id=0, has_side_effects=True, vmem_limit_bytes=60 * 1024 * 1024
        ),
        cost_estimate=pl.CostEstimate(
            flops=6 * rows * D * H, bytes_accessed=8 * D * H, transcendentals=rows * H
        ),
    )(ids, share, tokens, grads, up, down, local, momentum)


def tail_kernel(
    R, sel_ref, res_ref, outer_ref, local_ref, mom_ref, grad_ref, new_ref, moved_ref, copy_ref
):
    r = lax.axis_index("replica")
    width = mom_ref.shape[-1]
    grad_ref[...] = dot_nn(sel_ref[:, :CAP], res_ref[...]).astype(jnp.bfloat16)
    for one in range(R):
        cols = slice(one * width, (one + 1) * width)
        outer = outer_ref[:, cols]
        pseudo = outer - local_ref[0, :, cols]
        for other in range(1, R):
            pseudo = pseudo + (outer - local_ref[other, :, cols])
        pseudo = pseudo / R
        moved = outer_beta * mom_ref[one] + pseudo
        new_outer = outer - outer_rate * (pseudo + outer_beta * moved)
        new_ref[:, cols] = new_outer
        copy_ref[:, cols] = new_outer.astype(jnp.bfloat16)

        @pl.when(r == one)
        def _():
            moved_ref[...] = moved


def tail(R, sel, result, outer, local_all, mom_all):
    T = sel.shape[0]
    D = result.shape[1]
    rows, keys = outer.shape
    width = mom_all.shape[2]
    G = TAIL_STEPS
    few, cols = rows // G, D // G
    return pl.pallas_call(
        functools.partial(tail_kernel, R),
        grid=(G,),
        out_shape=(
            jax.ShapeDtypeStruct((T, D), jnp.bfloat16),
            jax.ShapeDtypeStruct((rows, keys), jnp.float32),
            jax.ShapeDtypeStruct((rows, width), jnp.float32),
            jax.ShapeDtypeStruct((rows, keys), jnp.bfloat16),
        ),
        in_specs=[
            pl.BlockSpec((T, T), lambda g: (0, 0)),
            pl.BlockSpec((CAP, cols), lambda g: (0, g)),
            pl.BlockSpec((few, keys), lambda g: (g, 0)),
            pl.BlockSpec((R, few, keys), lambda g: (0, g, 0)),
            pl.BlockSpec((R, few, width), lambda g: (0, g, 0)),
        ],
        out_specs=(
            pl.BlockSpec((T, cols), lambda g: (0, g)),
            pl.BlockSpec((few, keys), lambda g: (g, 0)),
            pl.BlockSpec((few, width), lambda g: (g, 0)),
            pl.BlockSpec((few, keys), lambda g: (g, 0)),
        ),
        compiler_params=pltpu.CompilerParams(vmem_limit_bytes=60 * 1024 * 1024),
    )(sel, result, outer, local_all, mom_all)


def per_device(
    R,
    F,
    tokens,
    grad_out,
    expert_ids,
    gate_share,
    up_weight,
    down_weight,
    local_keys,
    outer_keys,
    momentum,
):
    result, sel, local_all, mom_all = exchange(
        R,
        F,
        expert_ids[0].T,
        gate_share,
        tokens[0],
        grad_out[0],
        up_weight[0],
        down_weight[0],
        local_keys[0],
        momentum,
    )
    input_grad, new_outer, new_momentum, outer_copy = tail(
        R, sel, result, outer_keys, local_all, mom_all
    )
    return (input_grad[None], new_outer, new_momentum, outer_copy)


def solution(mesh):
    placed = (
        P("replica", "fsdp", None),
        P("replica", "fsdp", None),
        P("replica", "fsdp", None),
        P("replica", "fsdp"),
        P("replica", None, "fsdp"),
        P("replica", "fsdp", None),
        P("replica", "fsdp", None),
        P("fsdp", None),
        P("fsdp", "replica"),
    )
    return jax.shard_map(
        functools.partial(per_device, mesh.shape["replica"], mesh.shape["fsdp"]),
        mesh=mesh,
        in_specs=placed,
        out_specs=(
            P("replica", "fsdp", None),
            P("fsdp", None),
            P("fsdp", "replica"),
            P("fsdp", None),
        ),
        check_vma=False,
    )
```

```python
import functools

import jax
import jax.numpy as jnp
from jax import lax
from jax.experimental import pallas as pl
from jax.experimental.pallas import tpu as pltpu
from jax.sharding import PartitionSpec as P

CAP = 16
MAJOR = 4
PIECES = 8
BACK_PIECES = 6
KEY_ROWS = 48
TAIL_STEPS = 1

outer_beta = 0.9
outer_rate = 0.7

MESH = pl.DeviceIdType.MESH


def dot_nn(left, right):
    return jnp.dot(left, right, preferred_element_type=jnp.float32)


def dot_nt(left, right):
    return lax.dot_general(
        left, right, (((1,), (1,)), ((), ())), preferred_element_type=jnp.float32
    )


def staged(count, stages):
    def step(t, carry):
        for lag, stage in stages:
            piece = t - lag

            @pl.when((piece >= 0) & (piece < count))
            def _():
                stage(piece)

        return carry

    lax.fori_loop(0, count + max(lag for lag, _ in stages), step, 0)


def kernel(
    R,
    A,
    B,
    K,
    KR,
    ids_ref,
    share_ref,
    tok_ref,
    grad_ref,
    up_ref,
    down_ref,
    local_ref,
    mom_ref,
    res_ref,
    sel_out_ref,
    local_all,
    mom_all,
    src,
    buf,
    upv,
    downv,
    sel_ref,
    coef_ref,
    pre_ref,
    back_ref,
    hid_ref,
    part,
    sib_out,
    sib_in,
    x_out,
    x_in,
    z_out,
    z_in,
    src_sem,
    up_sem,
    down_sem,
    own_sem,
    y_send,
    y_recv,
    gz_send,
    gz_recv,
    go_send,
    go_recv,
    gx_send,
    gx_recv,
    gs_send,
    gs_recv,
    rs_send,
    rs_recv,
    rx_send,
    rx_recv,
    rz_send,
    rz_recv,
):
    r = lax.axis_index("replica")
    me = lax.axis_index("fsdp")
    c = lax.rem(me, 2)
    b = lax.rem(me // 2, B)
    a = me // (2 * B)
    NP = 2 * K
    width = src.shape[-1]
    column = A * CAP
    half = B * column

    def at(a_, b_, c_):
        return (r, (a_ * B + b_) * 2 + c_)

    sibling = at(a, b, 1 - c)
    z_peers = [at(lax.rem(a + j, A), b, c) for j in range(1, A)]
    x_peers = [at(a, lax.rem(b + j, B), c) for j in range(1, B)]
    y_peers = [(lax.rem(r + j, R), me) for j in range(1, R)]

    for k in range(K):
        cols = pl.ds(k * width, width)
        pltpu.make_async_copy(tok_ref.at[:, cols], src.at[k], src_sem.at[k]).start()
    for k in range(K):
        cols = pl.ds(k * width, width)
        pltpu.make_async_copy(up_ref.at[cols], upv.at[cols], up_sem.at[k]).start()
    for k in range(K):
        cols = pl.ds(k * width, width)
        pltpu.make_async_copy(grad_ref.at[:, cols], src.at[K + k], src_sem.at[K + k]).start()
    for k in range(K):
        cols = pl.ds(k * width, width)
        pltpu.make_async_copy(down_ref.at[:, cols], downv.at[k], down_sem.at[k]).start()
    own_local = pltpu.make_async_copy(local_ref, local_all.at[r], own_sem.at[0])
    own_mom = pltpu.make_async_copy(mom_ref, mom_all.at[r], own_sem.at[1])
    own_local.start()
    own_mom.start()

    barrier = pltpu.get_barrier_semaphore()
    peers = [sibling] + z_peers + x_peers + y_peers
    for peer in peers:
        pl.semaphore_signal(barrier, inc=1, device_id=peer, device_id_type=MESH)

    T = ids_ref.shape[1]
    first = (ids_ref[0:1, :] == 0).astype(jnp.float32)
    second = (ids_ref[1:2, :] == 0).astype(jnp.float32)
    named = jnp.broadcast_to(first + second, (T, T)).T
    row = lax.broadcasted_iota(jnp.int32, (T, T), 0)
    col = lax.broadcasted_iota(jnp.int32, (T, T), 1)
    below = jnp.where(col < row, 1.0, 0.0).astype(jnp.bfloat16)
    rank = dot_nn(below, named.astype(jnp.bfloat16))
    sel_t = jnp.where((rank == col.astype(jnp.float32)) & (named > 0.5), 1.0, 0.0)
    sel_out_ref[...] = sel_t.astype(jnp.bfloat16)
    sel = sel_t.T
    sel_ref[...] = sel[:CAP].astype(jnp.bfloat16)
    share = share_ref[...]
    coef = jnp.where(first > 0.5, share, 1.0 - share)
    coef_ref[...] = jnp.broadcast_to(
        jnp.sum(sel[:CAP] * coef, axis=1, keepdims=True), coef_ref.shape
    )
    pre_ref[...] = jnp.zeros_like(pre_ref)
    back_ref[...] = jnp.zeros_like(back_ref)

    pl.semaphore_wait(barrier, len(peers))

    def remote(source, target, send, recv, peer):
        return pltpu.make_async_remote_copy(
            src_ref=source,
            dst_ref=target,
            send_sem=send,
            recv_sem=recv,
            device_id=peer,
            device_id_type=MESH,
        )

    def rows_of(b_):
        return pl.ds(pl.multiple_of((c * B + b_) * column, column), column)

    def place(b_, k):
        return pl.ds(pl.multiple_of((c * B + b_) * column + k * CAP, CAP), CAP)

    def gz(p):
        return [
            remote(buf.at[p, place(b, 0)], buf.at[p, place(b, A - 1 - j)], gz_send.at[p, j], gz_recv.at[p, j], z_peers[j])
            for j in range(A - 1)
        ]

    def gx_own(p):
        mine = buf.at[p, place(b, 0)]
        return [
            remote(mine, mine, go_send.at[p, j], go_recv.at[p, j], x_peers[j])
            for j in range(B - 1)
        ]

    def gx(p):
        rows = pl.ds(pl.multiple_of((c * B + b) * column + CAP, CAP), column - CAP)
        rest = buf.at[p, rows]
        return [
            remote(rest, rest, gx_send.at[p, j], gx_recv.at[p, j], x_peers[j])
            for j in range(B - 1)
        ]

    def gs(p, j):
        part_of = buf.at[p, rows_of(lax.rem(b + j, B))]
        return remote(part_of, part_of, gs_send.at[p, j], gs_recv.at[p, j], sibling)

    key_pieces = local_ref.shape[0] // KEY_ROWS

    def ys(p):
        rows = pl.ds(pl.multiple_of(p * KEY_ROWS, 8), KEY_ROWS)
        copies = []
        for j in range(R - 1):
            copies.append(
                remote(local_ref.at[rows], local_all.at[r, rows], y_send.at[p, j, 0], y_recv.at[p, j, 0], y_peers[j])
            )
            copies.append(
                remote(mom_ref.at[rows], mom_all.at[r, rows], y_send.at[p, j, 1], y_recv.at[p, j, 1], y_peers[j])
            )
        return copies

    def pick(p):
        pltpu.make_async_copy(tok_ref.at[:, pl.ds(0, width)], src.at[p], src_sem.at[p]).wait()
        buf[p, place(b, 0), :] = dot_nn(sel_ref[...], src[p]).astype(jnp.bfloat16)
        for copy in gx_own(p) + gz(p):
            copy.start()

    def keys(p):
        @pl.when(p < key_pieces)
        def _():
            for copy in ys(p):
                copy.start()

    def across(p):
        for copy in gz(p):
            copy.wait_recv()
        for copy in gx(p):
            copy.start()
        gs(p, 0).start()

    def aside(p):
        for j in range(B - 1):
            gx_own(p)[j].wait_recv()
            gx(p)[j].wait_recv()
            gs(p, B - 1 - j).start()

    def multiply(p):
        for j in range(B):
            gs(p, j).wait_recv()

        @pl.when(p < K)
        def _():
            rows = pl.ds(pl.multiple_of(p * width, width), width)
            pltpu.make_async_copy(up_ref.at[pl.ds(0, width)], upv.at[rows], up_sem.at[p]).wait()
            pre_ref[...] += dot_nn(buf[p], upv[rows, :])

        @pl.when(p >= K)
        def _():
            k = p - K
            pltpu.make_async_copy(
                down_ref.at[:, pl.ds(0, width)], downv.at[k], down_sem.at[k]
            ).wait()
            back_ref[...] += dot_nt(buf[p], downv[k])

    def sent(p):
        for copy in gz(p) + gx_own(p) + gx(p) + [gs(p, j) for j in range(B)]:
            copy.wait_send()

    staged(NP, [(0, pick), (2, across), (2, keys), (4, aside), (6, multiply), (7, sent)])

    pre = pre_ref[...]
    sig = jax.nn.sigmoid(pre)
    hid_ref[...] = (back_ref[...] * sig * (1.0 + pre * (1.0 - sig))).astype(jnp.bfloat16)

    wide = part.shape[-1]
    own_half = pl.ds(pl.multiple_of(c * half, half), half)
    other_half = pl.ds(pl.multiple_of((1 - c) * half, half), half)

    def rs(q):
        return remote(sib_out.at[q], sib_in.at[q], rs_send.at[q], rs_recv.at[q], sibling)

    def rx(q):
        return [
            remote(x_out.at[q, j], x_in.at[q, j], rx_send.at[q, j], rx_recv.at[q, j], x_peers[j])
            for j in range(B - 1)
        ]

    def rz(q):
        return [
            remote(z_out.at[q, j], z_in.at[q, j], rz_send.at[q, j], rz_recv.at[q, j], z_peers[j])
            for j in range(A - 1)
        ]

    def produce(q):
        rows = pl.ds(pl.multiple_of(q * wide, wide), wide)
        part[q] = dot_nt(hid_ref[...], upv[rows, :])
        sib_out[q] = part[q, other_half, :].astype(jnp.bfloat16)
        rs(q).start()

    def pair(q):
        rs(q).wait_recv()
        for j, copy in enumerate(rx(q)):
            b_ = lax.rem(b + j + 1, B)
            there = pl.ds(pl.multiple_of(b_ * column, column), column)
            mine = part[q, pl.ds(pl.multiple_of(c * half + b_ * column, column), column), :]
            x_out[q, j] = (mine + sib_in[q, there, :].astype(jnp.float32)).astype(jnp.bfloat16)
            copy.start()

    def chain(q):
        here = pl.ds(pl.multiple_of(b * column, column), column)
        mine = pl.ds(pl.multiple_of(c * half + b * column, column), column)
        total = part[q, mine, :] + sib_in[q, here, :].astype(jnp.float32)
        for j, copy in enumerate(rx(q)):
            copy.wait_recv()
            total = total + x_in[q, j].astype(jnp.float32)
        part[q, mine, :] = total
        for j, copy in enumerate(rz(q)):
            z_out[q, j] = part[q, place(b, j + 1), :].astype(jnp.bfloat16)
            copy.start()

    def finish(q):
        total = part[q, place(b, 0), :]
        for j, copy in enumerate(rz(q)):
            copy.wait_recv()
            total = total + z_in[q, j].astype(jnp.float32)
        cols = pl.ds(pl.multiple_of(q * wide, 128), wide)
        res_ref[:, cols] = (coef_ref[:, 0:1] * total).astype(jnp.bfloat16)

    def returned(q):
        for copy in [rs(q)] + rx(q) + rz(q):
            copy.wait_send()

    staged(KR, [(0, produce), (1, pair), (2, chain), (4, finish), (5, returned)])

    def keys_done(p, carry):
        for copy in ys(p):
            copy.wait()
        return carry

    lax.fori_loop(0, key_pieces, keys_done, 0)
    own_local.wait()
    own_mom.wait()


def exchange(R, F, ids, share, tokens, grads, up, down, local, momentum):
    A = MAJOR
    B = F // (2 * A)
    K = PIECES
    KR = BACK_PIECES
    D = tokens.shape[1]
    H = up.shape[1]
    T = tokens.shape[0]
    width = D // K
    wide = D // KR
    rows = F * CAP
    column = A * CAP
    half = B * column
    dma = pltpu.SemaphoreType.DMA
    vmem = pl.BlockSpec(memory_space=pltpu.VMEM)
    hbm = pl.BlockSpec(memory_space=pl.ANY)
    return pl.pallas_call(
        functools.partial(kernel, R, A, B, K, KR),
        out_shape=(
            jax.ShapeDtypeStruct((CAP, D), jnp.bfloat16),
            jax.ShapeDtypeStruct((T, T), jnp.bfloat16),
            jax.ShapeDtypeStruct((R,) + local.shape, jnp.float32),
            jax.ShapeDtypeStruct((R,) + momentum.shape, jnp.float32),
        ),
        in_specs=[vmem, vmem, hbm, hbm, hbm, hbm, hbm, hbm],
        out_specs=(vmem, vmem, hbm, hbm),
        scratch_shapes=[
            pltpu.VMEM((2 * K, T, width), jnp.bfloat16),
            pltpu.VMEM((2 * K, rows, width), jnp.bfloat16),
            pltpu.VMEM((D, H), jnp.bfloat16),
            pltpu.VMEM((K, H, width), jnp.bfloat16),
            pltpu.VMEM((CAP, T), jnp.bfloat16),
            pltpu.VMEM((CAP, 128), jnp.float32),
            pltpu.VMEM((rows, H), jnp.float32),
            pltpu.VMEM((rows, H), jnp.float32),
            pltpu.VMEM((rows, H), jnp.bfloat16),
            pltpu.VMEM((KR, rows, wide), jnp.float32),
            pltpu.VMEM((KR, half, wide), jnp.bfloat16),
            pltpu.VMEM((KR, half, wide), jnp.bfloat16),
            pltpu.VMEM((KR, B - 1, column, wide), jnp.bfloat16),
            pltpu.VMEM((KR, B - 1, column, wide), jnp.bfloat16),
            pltpu.VMEM((KR, A - 1, CAP, wide), jnp.bfloat16),
            pltpu.VMEM((KR, A - 1, CAP, wide), jnp.bfloat16),
            dma((2 * K,)),
            dma((K,)),
            dma((K,)),
            dma((2,)),
            dma((local.shape[0] // KEY_ROWS, R - 1, 2)),
            dma((local.shape[0] // KEY_ROWS, R - 1, 2)),
            dma((2 * K, A - 1)),
            dma((2 * K, A - 1)),
            dma((2 * K, B - 1)),
            dma((2 * K, B - 1)),
            dma((2 * K, B - 1)),
            dma((2 * K, B - 1)),
            dma((2 * K, B)),
            dma((2 * K, B)),
            dma((KR,)),
            dma((KR,)),
            dma((KR, B - 1)),
            dma((KR, B - 1)),
            dma((KR, A - 1)),
            dma((KR, A - 1)),
        ],
        compiler_params=pltpu.CompilerParams(
            collective_id=0, has_side_effects=True, vmem_limit_bytes=60 * 1024 * 1024
        ),
        cost_estimate=pl.CostEstimate(
            flops=6 * rows * D * H, bytes_accessed=8 * D * H, transcendentals=rows * H
        ),
    )(ids, share, tokens, grads, up, down, local, momentum)


def tail_kernel(
    R, sel_ref, res_ref, outer_ref, local_ref, mom_ref, grad_ref, new_ref, moved_ref, copy_ref
):
    r = lax.axis_index("replica")
    width = mom_ref.shape[-1]
    grad_ref[...] = dot_nn(sel_ref[:, :CAP], res_ref[...]).astype(jnp.bfloat16)
    for one in range(R):
        cols = slice(one * width, (one + 1) * width)
        outer = outer_ref[:, cols]
        pseudo = outer - local_ref[0, :, cols]
        for other in range(1, R):
            pseudo = pseudo + (outer - local_ref[other, :, cols])
        pseudo = pseudo / R
        moved = outer_beta * mom_ref[one] + pseudo
        new_outer = outer - outer_rate * (pseudo + outer_beta * moved)
        new_ref[:, cols] = new_outer
        copy_ref[:, cols] = new_outer.astype(jnp.bfloat16)

        @pl.when(r == one)
        def _():
            moved_ref[...] = moved


def tail(R, sel, result, outer, local_all, mom_all):
    T = sel.shape[0]
    D = result.shape[1]
    rows, keys = outer.shape
    width = mom_all.shape[2]
    G = TAIL_STEPS
    few, cols = rows // G, D // G
    return pl.pallas_call(
        functools.partial(tail_kernel, R),
        grid=(G,),
        out_shape=(
            jax.ShapeDtypeStruct((T, D), jnp.bfloat16),
            jax.ShapeDtypeStruct((rows, keys), jnp.float32),
            jax.ShapeDtypeStruct((rows, width), jnp.float32),
            jax.ShapeDtypeStruct((rows, keys), jnp.bfloat16),
        ),
        in_specs=[
            pl.BlockSpec((T, T), lambda g: (0, 0)),
            pl.BlockSpec((CAP, cols), lambda g: (0, g)),
            pl.BlockSpec((few, keys), lambda g: (g, 0)),
            pl.BlockSpec((R, few, keys), lambda g: (0, g, 0)),
            pl.BlockSpec((R, few, width), lambda g: (0, g, 0)),
        ],
        out_specs=(
            pl.BlockSpec((T, cols), lambda g: (0, g)),
            pl.BlockSpec((few, keys), lambda g: (g, 0)),
            pl.BlockSpec((few, width), lambda g: (g, 0)),
            pl.BlockSpec((few, keys), lambda g: (g, 0)),
        ),
        compiler_params=pltpu.CompilerParams(vmem_limit_bytes=60 * 1024 * 1024),
    )(sel, result, outer, local_all, mom_all)


def per_device(
    R,
    F,
    tokens,
    grad_out,
    expert_ids,
    gate_share,
    up_weight,
    down_weight,
    local_keys,
    outer_keys,
    momentum,
):
    result, sel, local_all, mom_all = exchange(
        R,
        F,
        expert_ids[0].T,
        gate_share,
        tokens[0],
        grad_out[0],
        up_weight[0],
        down_weight[0],
        local_keys[0],
        momentum,
    )
    input_grad, new_outer, new_momentum, outer_copy = tail(
        R, sel, result, outer_keys, local_all, mom_all
    )
    return (input_grad[None], new_outer, new_momentum, outer_copy)


def solution(mesh):
    placed = (
        P("replica", "fsdp", None),
        P("replica", "fsdp", None),
        P("replica", "fsdp", None),
        P("replica", "fsdp"),
        P("replica", None, "fsdp"),
        P("replica", "fsdp", None),
        P("replica", "fsdp", None),
        P("fsdp", None),
        P("fsdp", "replica"),
    )
    return jax.shard_map(
        functools.partial(per_device, mesh.shape["replica"], mesh.shape["fsdp"]),
        mesh=mesh,
        in_specs=placed,
        out_specs=(
            P("replica", "fsdp", None),
            P("fsdp", None),
            P("fsdp", "replica"),
            P("fsdp", None),
        ),
        check_vma=False,
    )
```
